128 devices in a mesh: tok: 16 (over x, z_hi, core), inc: 2 (over z_lo), outc: 4 (over y).
Axes of the slice: x: 4, y: 4, z: 4 (z_hi: 2, z_lo: 2; z = z_hi * 2 + z_lo), core: 2. Of those that a mesh axis runs over, the one named last changes fastest.
Arguments:
- activations: bfloat16 [2, 4096, 8192], P(None, 'tok', 'inc'), may hold values from -0.119628906 to 0.119628906
- student_out: bfloat16 [2, 4096, 4096], P(None, ('tok', 'inc'), 'outc'), may hold values from -6 to 6
- teacher_out: bfloat16 [2, 4096, 4096], P(None, ('tok', 'inc'), 'outc'), may hold values from -6 to 6
- weight: bfloat16 [2, 4096, 4096], P('inc', 'tok', 'outc'), may hold values from -0.0625 to 0.0625
Outputs:
- input_grad: bfloat16 [2, 4096, 8192], P(None, ('tok', 'outc'), 'inc')
- weight_grad: float32 [2, 4096, 4096], P('inc', 'tok', 'outc')
The draws below stay inside these ranges and needn't reach their ends.
All inputs are finite; a program needn't handle non-finite values.
Results may differ from the reference program's by a relative error of at most 0.0051.
Values may be sent and summed in bfloat16 or wider, within the bound.
No kernel may reach another device: no remote copies, remote signals or barrier semaphores. Data moves between devices by JAX's collectives and lax.ppermute only.
A program may use at most 128 MiB of HBM per device.

```python
import jax
import jax.numpy as jnp

DIN = 8192
DOUT = 4096
MB = 2
TOKENS = 4096
INGROUPS = 2
IN_BLK = 4096


def with_spikes(entries, key, source, target, shards_of, factor):
    owner, partner = [(jnp.arange(entries.shape[dim]) // (entries.shape[dim] // shards_of)).reshape([-1 if axis == dim else 1 for axis in range(entries.ndim)]) for dim in (source, target)]
    chosen = jax.random.permutation(key, shards_of)[partner]
    strong = (owner == chosen) | (owner == (partner + shards_of // 2) % shards_of)
    return jnp.where(strong, factor * entries, entries)


def block_levels(own_key, dims, split, low, top_value):
    gain, own = 1.0, jax.random.fold_in(own_key, 6)
    for axis_at, shards_of in split:
        steps = jnp.exp(jax.random.uniform(jax.random.fold_in(own, axis_at), (shards_of,), jnp.float32, low / len(split), top_value / len(split)))
        gain = gain * jnp.repeat(steps, dims[axis_at] // shards_of).reshape([-1 if axis == axis_at else 1 for axis in range(len(dims))])
    return gain


def gaussian(stream_key, dims, width, bound, pieces=(), dtype=jnp.bfloat16):
    result = jax.random.normal(stream_key, dims, jnp.float32) * width
    if len(pieces) > 0:
        result = block_levels(stream_key, dims, pieces, -0.22, 0.18) * result
    return jnp.clip(result, min=-bound, max=bound).astype(dtype)


def bell_draw_with(rng, dims, spread, reach, shards, heavy, held_as=jnp.bfloat16):
    drawn = spread * jax.random.normal(rng, dims, jnp.float32)
    if shards:
        drawn = drawn * block_levels(rng, dims, shards, -0.22, 0.18)
    return jnp.clip(with_spikes(drawn, jax.random.fold_in(rng, 3), *heavy), -reach, reach).astype(held_as)


def setup_inputs(seed: int = 0) -> dict:
    seeds = jax.random.split(jax.random.key(seed), 5)
    activations = bell_draw_with(seeds[0], (MB, TOKENS, DIN), 0.02, 0.119628906, ((1, 16), (2, 2)), (1, 2, 16, 2.0))
    student_out = gaussian(seeds[1], (MB, TOKENS, DOUT), 1.0, 6.0, ((1, 32), (2, 4)))
    teacher_out = gaussian(seeds[2], (MB, TOKENS, DOUT), 1.0, 6.0, ((1, 32), (2, 4)))
    weight = gaussian(seeds[3], (INGROUPS, IN_BLK, DOUT), DIN ** -0.5, 0.0625, ((0, 2), (1, 16), (2, 4)))
    return {"activations": activations, "student_out": student_out, "teacher_out": teacher_out, "weight": weight}


def reference(activations, student_out, teacher_out, weight):
    difference = (student_out.astype(jnp.float32) - teacher_out.astype(jnp.float32)).astype(jnp.bfloat16)
    full_weight = weight.reshape(INGROUPS * IN_BLK, DOUT)
    input_grad = jnp.einsum("mtc,rc->mtr", difference.astype(jnp.float32), full_weight.astype(jnp.float32)).astype(jnp.bfloat16)
    weight_grad = jnp.einsum("mti,mtc->ic", activations.astype(jnp.float32), difference.astype(jnp.float32))
    return input_grad, weight_grad.reshape(INGROUPS, IN_BLK, DOUT)
```

```python
import jax
import jax.numpy as jnp
from jax import lax
from jax.sharding import PartitionSpec as P

NX, NZ, NC, NY = 4, 2, 2, 4


def tok_of(x, zh, c):
    return ((x % NX) * NZ + zh) * NC + c


def over_tok(move):
    return [
        (tok_of(x, zh, c), tok_of(*move(x, zh, c)))
        for x in range(NX)
        for zh in range(NZ)
        for c in range(NC)
    ]


STEP_X = over_tok(lambda x, zh, c: (x + 1 - 2 * c, zh, c))
SWAP_ZH = over_tok(lambda x, zh, c: (x, 1 - zh, c))
SWAP_C = over_tok(lambda x, zh, c: (x, zh, 1 - c))
SWAP_ZL = [(0, 1), (1, 0)]
STEP_Y = [
    (k * NY + y, k * NY + (y + 1 - 2 * (k % NC)) % NY)
    for k in range(NX * NZ * NC)
    for y in range(NY)
]


def local(activations, student_out, teacher_out, weight):
    f32, bf16 = jnp.float32, jnp.bfloat16
    tok = lax.axis_index("tok")
    c, zh, x = tok % NC, (tok // NC) % NZ, tok // (NC * NZ)
    zl, y = lax.axis_index("inc"), lax.axis_index("outc")
    d = 1 - 2 * c
    own = weight[0]
    rows, cols = own.shape
    mb, toks, _ = activations.shape
    part = toks // NY

    def x_at(k):
        return (x + k * d + 4 * NX) % NX

    def y_at(k):
        return (y + k * d + 4 * NY) % NY

    def gather_x(first):
        buf = jnp.zeros((NX * rows, cols), bf16)
        piece = first
        buf = lax.dynamic_update_slice(buf, piece, (x * rows, 0))
        for s in range(1, NX):
            piece = lax.ppermute(piece, "tok", STEP_X)
            buf = lax.dynamic_update_slice(buf, piece, (x_at(-s) * rows, 0))
        return buf

    diff = (student_out.astype(f32) - teacher_out.astype(f32)).astype(bf16)
    diff_z = lax.ppermute(diff, "inc", SWAP_ZL)
    w_other = lax.ppermute(own, "tok", SWAP_ZH)
    w_o = gather_x(own)

    def act_piece(k, core):
        return lax.dynamic_slice(
            activations, (0, 0, (k * NC + core) * rows), (mb, toks, rows)
        )

    act_send = jnp.stack([act_piece(k, 1 - c) for k in range(NX * NZ)])
    act_got = lax.ppermute(act_send, "tok", SWAP_C)

    mine = jnp.where(
        zl == 0,
        jnp.concatenate([diff, diff_z], axis=1),
        jnp.concatenate([diff_z, diff], axis=1),
    )
    theirs = lax.ppermute(mine, "tok", SWAP_C)
    w_p = gather_x(w_other)

    def dw_part(xt, zt):
        k = xt * NZ + zt
        got = lax.dynamic_index_in_dim(act_got, k, 0, keepdims=False)
        return jnp.einsum(
            "mtr,mtc->rc", act_piece(k, c), mine, preferred_element_type=f32
        ) + jnp.einsum("mtr,mtc->rc", got, theirs, preferred_element_type=f32)

    def dw_ring(zt):
        send = dw_part(x_at(3), zt).astype(bf16)
        for k in (2, 1, 0):
            got = lax.ppermute(send, "tok", STEP_X)
            total = dw_part(x_at(k), zt) + got.astype(f32)
            send = total.astype(bf16)
        return total

    def dx_part(yt, w):
        a = lax.dynamic_slice(mine, (0, yt * part, 0), (mb, part, cols))
        b = lax.dynamic_slice(theirs, (0, yt * part, 0), (mb, part, cols))
        both = jnp.concatenate([a, b]).reshape(2 * mb * part, cols)
        return jnp.einsum("tc,rc->tr", both, w, preferred_element_type=f32)

    def dx_ring(w):
        send = dx_part(y_at(3), w).astype(bf16)
        for k in (2, 1, 0):
            got = lax.ppermute(send, ("tok", "outc"), STEP_Y)
            send = (dx_part(y_at(k), w) + got.astype(f32)).astype(bf16)
        return send

    dw_p = dw_ring(1 - zh)
    dw_cross = lax.ppermute(dw_p.astype(bf16), "tok", SWAP_ZH)
    dw_o = dw_ring(zh)
    weight_grad = dw_o + dw_cross.astype(f32)

    half = mb * part
    dx_o, dx_p = dx_ring(w_o), dx_ring(w_p)
    got_o = lax.ppermute(dx_o[half:], "tok", SWAP_C)
    got_p = lax.ppermute(dx_p[half:], "tok", SWAP_C)
    dx_o, dx_p = dx_o[:half], dx_p[:half]
    pieces = []
    for xt in range(NX):
        at = slice(xt * rows, (xt + 1) * rows)
        for zt in range(NZ):
            here = jnp.where(zh == zt, dx_o[:, at], dx_p[:, at])
            there = jnp.where(zh == zt, got_o[:, at], got_p[:, at])
            pieces += [jnp.where(c == 0, here, there), jnp.where(c == 0, there, here)]
    input_grad = jnp.concatenate(pieces, axis=1).reshape(mb, part, -1)
    return input_grad, weight_grad.reshape(weight.shape)


def solution(mesh):
    placed = (
        P(None, "tok", "inc"),
        P(None, ("tok", "inc"), "outc"),
        P(None, ("tok", "inc"), "outc"),
        P("inc", "tok", "outc"),
    )
    return jax.shard_map(
        local,
        mesh=mesh,
        in_specs=placed,
        out_specs=(P(None, ("tok", "outc"), "inc"), P("inc", "tok", "outc")),
        check_vma=False,
    )
```

```python
import functools

import jax
import jax.numpy as jnp
from jax import lax
from jax.experimental import pallas as pl
from jax.experimental.pallas import tpu as pltpu
from jax.sharding import Mesh
from jax.sharding import PartitionSpec as P

NX, NZ, NC, NL, NY = 4, 2, 2, 2, 4
F32, BF16 = jnp.float32, jnp.bfloat16


def cost(flops, *arrays):
    moved = sum(a.size * a.dtype.itemsize for a in arrays)
    return pl.CostEstimate(flops=flops, bytes_accessed=moved, transcendentals=0)


def other_columns(act, c):
    mb, toks, width = act.shape
    n = NX * NZ
    rows = width // (n * NC)

    def body(core, a_ref, out_ref):
        out_ref[0] = a_ref[...]

    out = jax.ShapeDtypeStruct((n, mb, toks, rows), act.dtype)
    return pl.pallas_call(
        body,
        out_shape=out,
        grid_spec=pltpu.PrefetchScalarGridSpec(
            num_scalar_prefetch=1,
            grid=(n,),
            in_specs=[
                pl.BlockSpec(
                    (mb, toks, rows), lambda k, core: (0, 0, k * NC + 1 - core[0])
                )
            ],
            out_specs=pl.BlockSpec((1, mb, toks, rows), lambda k, core: (k, 0, 0, 0)),
        ),
        cost_estimate=cost(0, out, out),
        name="other_columns",
    )(c.reshape(1), act)


def dw_body(n, n_add, at, *refs):
    zl = at[0]
    mine, refs = refs[:n], refs[n:]
    theirs, refs = refs[:n], refs[n:]
    diffs, refs = refs[:4], refs[4:]
    adds, outs = refs[:n_add], refs[n_add:]
    mb, part, cols = diffs[0].shape
    for k in range(n):
        total = None
        for j, diff in enumerate(diffs):
            start = pl.multiple_of((zl if j % 2 == 0 else 1 - zl) * part, part)
            if j < 2:
                a = mine[k][:, pl.ds(start, part), :]
            else:
                a = theirs[k][0, :, pl.ds(start, part), :]
            term = lax.dot_general(
                a.reshape(mb * part, a.shape[-1]),
                diff[...].reshape(mb * part, cols),
                (((0,), (0,)), ((), ())),
                preferred_element_type=F32,
            )
            total = term if total is None else total + term
        for add in adds:
            total = total + add[...].astype(F32)
        outs[k][...] = total.astype(outs[k].dtype)


def dw_sums(act, act_got, diffs, chunks, c, zl, adds=(), dtype=BF16):
    mb, toks, width = act.shape
    rows = width // (NX * NZ * NC)
    cols = diffs[0].shape[-1]
    n, steps = len(chunks), 2
    wide = cols // steps
    at = jnp.stack([zl, *(k * NC + c for k in chunks), *chunks])
    out = jax.ShapeDtypeStruct((rows, cols), dtype)

    def column(k):
        return pl.BlockSpec((mb, toks, rows), lambda i, at: (0, 0, at[1 + k]))

    def chunk(k):
        return pl.BlockSpec((1, mb, toks, rows), lambda i, at: (at[1 + n + k], 0, 0, 0))

    diff_spec = pl.BlockSpec((mb, toks // 2, wide), lambda i, at: (0, 0, i))
    flat_spec = pl.BlockSpec((rows, wide), lambda i, at: (0, i))
    return pl.pallas_call(
        functools.partial(dw_body, n, len(adds)),
        out_shape=[out] * n,
        grid_spec=pltpu.PrefetchScalarGridSpec(
            num_scalar_prefetch=1,
            grid=(steps,),
            in_specs=[
                *(column(k) for k in range(n)),
                *(chunk(k) for k in range(n)),
                *([diff_spec] * 4),
                *([flat_spec] * len(adds)),
            ],
            out_specs=[flat_spec] * n,
        ),
        cost_estimate=cost(4 * n * mb * toks * rows * cols, *diffs, *([out] * n)),
        name="dw_sums",
    )(at, *([act] * n), *([act_got] * n), *diffs, *adds)


def dx_body(at, *refs):
    diffs, pieces, out = refs[:4], refs[4:8], refs[8]
    c, zl = at[0], at[1]
    _, part, cols = diffs[0].shape
    rows = pieces[0].shape[0]
    half = part // 2
    for p, piece in enumerate(pieces):
        w = piece[...]
        lanes = pl.ds(pl.multiple_of(at[2 + p] * rows, rows), rows)
        for j, diff in enumerate(diffs):
            got = lax.dot_general(
                diff[0], w, (((1,), (1,)), ((), ())), preferred_element_type=F32
            ).astype(BF16)
            core = c if j < 2 else 1 - c
            first = core * NY + 2 * (zl if j % 2 == 0 else 1 - zl)
            for h in range(2):
                out[first + h, :, lanes] = got[h * half : (h + 1) * half]


def dx_sums(diffs, pieces, where, c, zl):
    mb, part, cols = diffs[0].shape
    rows = pieces[0].shape[0]
    half = part // 2
    out = jax.ShapeDtypeStruct((NC * NY, mb * half, NX * rows), BF16)
    return pl.pallas_call(
        dx_body,
        out_shape=out,
        grid_spec=pltpu.PrefetchScalarGridSpec(
            num_scalar_prefetch=1,
            grid=(mb,),
            in_specs=[
                *([pl.BlockSpec((1, part, cols), lambda m, at: (m, 0, 0))] * 4),
                *([pl.BlockSpec((rows, cols), lambda m, at: (0, 0))] * NX),
            ],
            out_specs=pl.BlockSpec(
                (NC * NY, half, NX * rows), lambda m, at: (0, m, 0)
            ),
        ),
        cost_estimate=cost(8 * mb * part * cols * NX * rows, out, *diffs, *pieces),
        name="dx_sums",
    )(jnp.stack([c, zl, *where]), *diffs, *pieces)


def join_body(at, o_ref, p_ref, out_ref):
    zh = at[0]
    width = o_ref.shape[-1]
    rows = width // NX
    for ref, z in ((o_ref, zh), (p_ref, 1 - zh)):
        for n in range(NC):
            total = ref[n * NY].astype(F32)
            for k in range(1, NY):
                total = total + ref[n * NY + k].astype(F32)
            total = total.astype(BF16)
            for xt in range(NX):
                start = ((xt * NZ + z) * NC + n) * rows
                lanes = pl.ds(pl.multiple_of(start, rows), rows)
                out_ref[0, :, lanes] = total[:, xt * rows : (xt + 1) * rows]


def join(got_o, got_p, zh, mb):
    n, toks, width = got_o.shape
    part = toks // mb
    out = jax.ShapeDtypeStruct((mb, part, NZ * NC * width), BF16)
    spec = pl.BlockSpec((n, part, width), lambda m, at: (0, m, 0))
    return pl.pallas_call(
        join_body,
        out_shape=out,
        grid_spec=pltpu.PrefetchScalarGridSpec(
            num_scalar_prefetch=1,
            grid=(mb,),
            in_specs=[spec, spec],
            out_specs=pl.BlockSpec((1, part, NZ * NC * width), lambda m, at: (m, 0, 0)),
        ),
        cost_estimate=cost(2 * got_o.size, got_o, got_p, out),
        name="join",
    )(zh.reshape(1), got_o, got_p)


def after(value, *others):
    return lax.optimization_barrier((value, *others))[0]


def by_x(k):
    return [(x, (x + k) % NX) for x in range(NX)]


STEP_X = [
    (x * NC + c, (x + 1 - 2 * c) % NX * NC + c) for x in range(NX) for c in range(NC)
]
SWAP = [(0, 1), (1, 0)]


def local(activations, student_out, teacher_out, weight):
    x, zh, c = (lax.axis_index(n) for n in ("x", "zh", "core"))
    zl = lax.axis_index("inc")
    d = 1 - 2 * c
    own = weight[0]
    mb = activations.shape[0]

    def x_at(k):
        return (x + k * d) & (NX - 1)

    def step_x(value):
        return lax.ppermute(value, ("x", "core"), STEP_X)

    def round_x(piece):
        below = lax.ppermute(piece, "x", by_x(1))
        above = lax.ppermute(piece, "x", by_x(-1))
        far = step_x(jnp.where(c == 0, below, above))
        return (piece, below, above, far), tuple((x + k) & 3 for k in (0, -1, 1, 2))

    diff = (student_out.astype(F32) - teacher_out.astype(F32)).astype(BF16)
    diff_z = lax.ppermute(diff, "inc", SWAP)
    w_z = lax.ppermute(own, "zh", SWAP)
    w_o, at_o = round_x(own)
    act_got = lax.ppermute(other_columns(activations, c), "core", SWAP)
    diffs = (
        diff,
        diff_z,
        lax.ppermute(diff, "core", SWAP),
        lax.ppermute(diff_z, "core", SWAP),
    )
    w_p, at_p = round_x(w_z)

    def dw(ks, z, adds=(), dtype=BF16):
        chunks = [x_at(k) * NZ + z for k in ks]
        return dw_sums(activations, act_got, diffs, chunks, c, zl, adds, dtype)

    def swap_zh(value):
        return lax.ppermute(value, "zh", SWAP)

    z = {}
    (part,) = dw((3,), 1 - zh)
    z[3] = swap_zh(part)
    for k, part in zip((2, 1, 0), dw((2, 1, 0), 1 - zh), strict=True):
        z[k] = swap_zh(part)
    (total,) = dw((3,), zh, (z[3],))
    for k in (2, 1, 0):
        got = step_x(total)
        (total,) = dw((k,), zh, (z[k], got), F32 if k == 0 else BF16)

    def over_y(pieces, where):
        partial = dx_sums(diffs, pieces, where, c, zl)
        return lax.all_to_all(partial, ("core", "outc"), 0, 0, tiled=True)

    input_grad = join(over_y(w_o, at_o), over_y(w_p, at_p), zh, mb)
    return input_grad, total.reshape(weight.shape)


def solution(mesh):
    fine = Mesh(
        mesh.devices.reshape(NX, NZ, NC, NL, NY), ("x", "zh", "core", "inc", "outc")
    )
    tok = ("x", "zh", "core")
    placed = (
        P(None, tok, "inc"),
        P(None, (*tok, "inc"), "outc"),
        P(None, (*tok, "inc"), "outc"),
        P("inc", tok, "outc"),
    )
    return jax.shard_map(
        local,
        mesh=fine,
        in_specs=placed,
        out_specs=(P(None, (*tok, "outc"), "inc"), P("inc", tok, "outc")),
        check_vma=False,
    )
```

```python
import jax
import jax.numpy as jnp
from jax import lax
from jax.experimental import pallas as pl
from jax.experimental.pallas import tpu as pltpu
from jax.sharding import Mesh
from jax.sharding import PartitionSpec as P

NX, NZ, NC, NL, NY = 4, 2, 2, 2, 4
F32, BF16 = jnp.float32, jnp.bfloat16
PIECES = (0, -1, 1, 2)


def cost(flops, *arrays):
    moved = sum(a.size * a.dtype.itemsize for a in arrays)
    return pl.CostEstimate(flops=flops, bytes_accessed=moved, transcendentals=0)


def split_columns(act, c):
    mb, toks, width = act.shape
    n = NX * NZ
    rows = width // (n * NC)

    def body(core, a_ref, mine_ref, other_ref):
        own = core[0] == 0
        first, second = a_ref[:, :, :rows], a_ref[:, :, rows:]
        mine_ref[0] = jnp.where(own, first, second)
        other_ref[0] = jnp.where(own, second, first)

    out = jax.ShapeDtypeStruct((n, mb, toks, rows), act.dtype)
    spec = pl.BlockSpec((1, mb, toks, rows), lambda k, core: (k, 0, 0, 0))
    return pl.pallas_call(
        body,
        out_shape=(out, out),
        grid_spec=pltpu.PrefetchScalarGridSpec(
            num_scalar_prefetch=1,
            grid=(n,),
            in_specs=[pl.BlockSpec((mb, toks, NC * rows), lambda k, core: (0, 0, k))],
            out_specs=[spec, spec],
        ),
        compiler_params=pltpu.CompilerParams(vmem_limit_bytes=8 << 20),
        cost_estimate=cost(0, act, act),
        name="split_columns",
    )(c.reshape(1), act)


def dx_body(core, mine, theirs, *refs):
    pieces, out, lhs = refs[:NX], refs[NX], refs[NX + 1]
    mb, toks, cols = mine.shape
    part = toks // NY
    rows = pieces[0].shape[0]
    for diff, n in ((mine, core[0]), (theirs, 1 - core[0])):
        for yt in range(NY):
            for m in range(mb):
                lhs[n, yt, m] = diff[m, yt * part : (yt + 1) * part]
    left = lhs[...].reshape(NC * NY * mb * part, cols)
    for p, piece in enumerate(pieces):
        got = lax.dot_general(
            left, piece[...], (((1,), (1,)), ((), ())), preferred_element_type=F32
        )
        got = got.astype(BF16).reshape(NC * NY, mb * part, rows)
        out[:, :, p * rows : (p + 1) * rows] = got


def dx_sums(mine, theirs, pieces, c):
    mb, toks, cols = mine.shape
    rows = pieces[0].shape[0]
    part = toks // NY
    out = jax.ShapeDtypeStruct((NC * NY, mb * part, NX * rows), BF16)
    vmem = pl.BlockSpec(memory_space=pltpu.VMEM)
    return pl.pallas_call(
        dx_body,
        out_shape=out,
        in_specs=[pl.BlockSpec(memory_space=pltpu.SMEM), *([vmem] * (2 + NX))],
        out_specs=vmem,
        scratch_shapes=[pltpu.VMEM((NC, NY, mb, part, cols), BF16)],
        compiler_params=pltpu.CompilerParams(vmem_limit_bytes=20 << 20),
        cost_estimate=cost(4 * out.size * cols, out, mine, theirs, *pieces),
        name="dx_sums",
    )(c.reshape(1), mine, theirs, *pieces)


def join_body(at, o_ref, p_ref, out_ref):
    x, zh = at[0], at[1]
    width = o_ref.shape[-1]
    rows = width // NX
    for ref, z in ((o_ref, zh), (p_ref, 1 - zh)):
        for n in range(NC):
            total = ref[n * NY].astype(F32)
            for k in range(1, NY):
                total = total + ref[n * NY + k].astype(F32)
            total = total.astype(BF16)
            for p, away in enumerate(PIECES):
                start = ((((x + away) & (NX - 1)) * NZ + z) * NC + n) * rows
                lanes = pl.ds(pl.multiple_of(start, rows), rows)
                out_ref[0, :, lanes] = total[:, p * rows : (p + 1) * rows]


def join(got_o, got_p, x, zh, mb):
    n, toks, width = got_o.shape
    part = toks // mb
    out = jax.ShapeDtypeStruct((mb, part, NZ * NC * width), BF16)
    spec = pl.BlockSpec((n, part, width), lambda m, at: (0, m, 0))
    return pl.pallas_call(
        join_body,
        out_shape=out,
        grid_spec=pltpu.PrefetchScalarGridSpec(
            num_scalar_prefetch=1,
            grid=(mb,),
            in_specs=[spec, spec],
            out_specs=pl.BlockSpec((1, part, NZ * NC * width), lambda m, at: (m, 0, 0)),
        ),
        compiler_params=pltpu.CompilerParams(vmem_limit_bytes=16 << 20),
        cost_estimate=cost(2 * got_o.size, got_o, got_p, out),
        name="join",
    )(jnp.stack([x, zh]), got_o, got_p)


def after(value, *others):
    return lax.optimization_barrier((value, *others))[0]


def by_x(k):
    return [(x, (x + k) % NX) for x in range(NX)]


STEP_X, BACK_X = (
    [
        (x * NC + c, (x + way * (1 - 2 * c)) % NX * NC + c)
        for x in range(NX)
        for c in range(NC)
    ]
    for way in (1, -1)
)
SWAP = [(0, 1), (1, 0)]


def local(activations, student_out, teacher_out, weight):
    x, zh, c = (lax.axis_index(n) for n in ("x", "zh", "core"))
    zl = lax.axis_index("inc")
    d = 1 - 2 * c
    own = weight[0]
    mb = activations.shape[0]

    def step_x(value):
        return lax.ppermute(value, ("x", "core"), STEP_X)

    def back_x(value):
        return lax.ppermute(value, ("x", "core"), BACK_X)

    def swap_zh(value):
        return lax.ppermute(value, "zh", SWAP)

    def round_x(piece):
        below = lax.ppermute(piece, "x", by_x(1))
        above = lax.ppermute(piece, "x", by_x(-1))
        return piece, below, above, step_x(jnp.where(c == 0, below, above))

    diff = (student_out.astype(F32) - teacher_out.astype(F32)).astype(BF16)
    diff_z = lax.ppermute(diff, "inc", SWAP)
    w_o = round_x(own)
    w_z = swap_zh(after(own, diff_z))
    act_mine, act_send = split_columns(after(activations, diff), c)
    act_got = lax.ppermute(act_send, "core", SWAP)
    diff_z = after(diff_z, w_o[1], w_o[2])
    mine = jnp.where(
        zl == 0,
        jnp.concatenate([diff, diff_z], axis=1),
        jnp.concatenate([diff_z, diff], axis=1),
    )
    theirs = lax.ppermute(mine, "core", SWAP)

    def dw(k, z, *got):
        at = ((x + k * d) & (NX - 1)) * NZ + z
        total = None
        for act, part in ((act_mine, mine), (act_got, theirs)):
            a = lax.dynamic_index_in_dim(act, at, 0, keepdims=False)
            term = jnp.einsum("mtr,mtc->rc", a, part, preferred_element_type=F32)
            total = term if total is None else total + term
        for g in got:
            total = total + g.astype(F32)
        return total

    p, o = 1 - zh, zh
    send_p, send_o = dw(2, p).astype(BF16), dw(2, o).astype(BF16)
    far_p, far_o = step_x(send_p), step_x(send_o)

    def over_y(partial):
        return lax.all_to_all(partial, ("core", "outc"), 0, 0, tiled=True)

    partial_o = dx_sums(mine, after(theirs, send_p, send_o), w_o, c)
    got_o = over_y(partial_o)
    mine, theirs, act_got, w_z = lax.optimization_barrier(
        (mine, theirs, act_got, w_z, partial_o)
    )[:4]
    w_p = round_x(w_z)
    back_p = back_x(dw(-1, p).astype(BF16))
    fwd_p = step_x(dw(1, p, far_p).astype(BF16))
    back_o = back_x(dw(-1, o).astype(BF16))
    fwd_o = step_x(dw(1, o, far_o).astype(BF16))
    cross = swap_zh(dw(0, p, back_p, fwd_p).astype(BF16))
    weight_grad = dw(0, o, back_o, fwd_o) + cross.astype(F32)

    partial_p = dx_sums(mine, theirs, w_p, c)
    got_p = over_y(after(partial_p, got_o))
    input_grad = join(got_o, got_p, x, zh, mb)
    return input_grad, weight_grad.reshape(weight.shape)


def solution(mesh):
    fine = Mesh(
        mesh.devices.reshape(NX, NZ, NC, NL, NY), ("x", "zh", "core", "inc", "outc")
    )
    tok = ("x", "zh", "core")
    placed = (
        P(None, tok, "inc"),
        P(None, (*tok, "inc"), "outc"),
        P(None, (*tok, "inc"), "outc"),
        P("inc", tok, "outc"),
    )
    return jax.shard_map(
        local,
        mesh=fine,
        in_specs=placed,
        out_specs=(P(None, (*tok, "outc"), "inc"), P("inc", tok, "outc")),
        check_vma=False,
    )
```

```python
import jax
import jax.numpy as jnp
from jax import lax
from jax.experimental import pallas as pl
from jax.experimental.pallas import tpu as pltpu
from jax.sharding import Mesh
from jax.sharding import PartitionSpec as P

NX, NZ, NC, NL, NY = 4, 2, 2, 2, 4
F32, BF16 = jnp.float32, jnp.bfloat16
PIECES = (0, -1, 1, 2)


def cost(flops, *arrays):
    moved = sum(a.size * a.dtype.itemsize for a in arrays)
    return pl.CostEstimate(flops=flops, bytes_accessed=moved, transcendentals=0)


def other_columns(act, c):
    mb, toks, width = act.shape
    n = NX * NZ
    rows = width // (n * NC)

    def body(core, a_ref, out_ref):
        pick = core[0] == 0
        out_ref[0] = jnp.where(pick, a_ref[:, :, rows:], a_ref[:, :, :rows])

    out = jax.ShapeDtypeStruct((n, mb, toks, rows), act.dtype)
    return pl.pallas_call(
        body,
        out_shape=out,
        grid_spec=pltpu.PrefetchScalarGridSpec(
            num_scalar_prefetch=1,
            grid=(n,),
            in_specs=[pl.BlockSpec((mb, toks, NC * rows), lambda k, core: (0, 0, k))],
            out_specs=pl.BlockSpec((1, mb, toks, rows), lambda k, core: (k, 0, 0, 0)),
        ),
        compiler_params=pltpu.CompilerParams(vmem_limit_bytes=8 << 20),
        cost_estimate=cost(0, act, out),
        name="other_columns",
    )(c.reshape(1), act)


def four_terms(rows, cols):
    return [jax.ShapeDtypeStruct((rows, cols), t) for t in (BF16, BF16, F32, F32)]


def dw_body(at, act, got, mine, theirs, *outs):
    mb, toks, cols = mine.shape
    rows = got.shape[-1]
    wide = cols // 2
    for k, out in enumerate(outs):
        lanes = pl.ds(pl.multiple_of((at[k] * NC + at[len(outs)]) * rows, rows), rows)
        a = act[:, :, lanes].reshape(mb * toks, rows)
        b = got[at[k]].reshape(mb * toks, rows)
        for j in range(0, cols, wide):
            total = None
            for lhs, diff in ((a, mine), (b, theirs)):
                term = lax.dot_general(
                    lhs,
                    diff[:, :, j : j + wide].reshape(mb * toks, wide),
                    (((0,), (0,)), ((), ())),
                    preferred_element_type=F32,
                )
                total = term if total is None else total + term
            out[:, j : j + wide] = total.astype(out.dtype)


def dw_terms(at, act, got, mine, theirs):
    outs = four_terms(got.shape[-1], mine.shape[-1])
    vmem = pl.BlockSpec(memory_space=pltpu.VMEM)
    return pl.pallas_call(
        dw_body,
        out_shape=outs,
        in_specs=[pl.BlockSpec(memory_space=pltpu.SMEM), *([vmem] * 4)],
        out_specs=[vmem] * 4,
        compiler_params=pltpu.CompilerParams(vmem_limit_bytes=6 << 20),
        cost_estimate=cost(16 * mine.size * got.shape[-1], *outs, mine, theirs, got),
        name="dw_terms",
    )(at, act, got, mine, theirs)


def dx_body(at, mine, theirs, *refs):
    pieces, outs, lhs = refs[:NX], refs[NX : NX + 4], refs[NX + 4]
    mb, toks, cols = mine.shape
    part = toks // NY
    rows = pieces[0].shape[0]
    for k in range(4):
        start = pl.multiple_of(at[k] * part, part)
        for n, diff in enumerate((mine, theirs)):
            for m in range(mb):
                lhs[k, n, m] = diff[m, pl.ds(start, part)]
    each = NC * mb * part
    left = lhs[...].reshape(4 * each, cols)
    for p, piece in enumerate(pieces):
        got = lax.dot_general(
            left, piece[...], (((1,), (1,)), ((), ())), preferred_element_type=F32
        )
        for k, out in enumerate(outs):
            term = got[k * each : (k + 1) * each]
            out[:, p * rows : (p + 1) * rows] = term.astype(out.dtype)


def dx_terms(at, mine, theirs, pieces):
    mb, toks, cols = mine.shape
    part = toks // NY
    outs = four_terms(NC * mb * part, NX * pieces[0].shape[0])
    vmem = pl.BlockSpec(memory_space=pltpu.VMEM)
    return pl.pallas_call(
        dx_body,
        out_shape=outs,
        in_specs=[pl.BlockSpec(memory_space=pltpu.SMEM), *([vmem] * (2 + NX))],
        out_specs=[vmem] * 4,
        scratch_shapes=[pltpu.VMEM((4, NC, mb, part, cols), BF16)],
        compiler_params=pltpu.CompilerParams(vmem_limit_bytes=8 << 20),
        cost_estimate=cost(8 * outs[0].size * cols, *outs, mine, theirs, *pieces),
        name="dx_terms",
    )(at, mine, theirs, *pieces)


def place_body(at, keep_o, got_o, keep_p, got_p, out_ref):
    x, zh, c = at[0], at[1], at[2]
    mb, part, _ = out_ref.shape
    rows = keep_o.shape[-1] // NX
    for ref, z, n in (
        (keep_o, zh, c),
        (got_o, zh, 1 - c),
        (keep_p, 1 - zh, c),
        (got_p, 1 - zh, 1 - c),
    ):
        for p, away in enumerate(PIECES):
            start = ((((x + away) & (NX - 1)) * NZ + z) * NC + n) * rows
            lanes = pl.ds(pl.multiple_of(start, rows), rows)
            for m in range(mb):
                out_ref[m, :, lanes] = ref[
                    m * part : (m + 1) * part, p * rows : (p + 1) * rows
                ]


def place(at, mb, *parts):
    toks, width = parts[0].shape
    out = jax.ShapeDtypeStruct((mb, toks // mb, NZ * NC * width), BF16)
    vmem = pl.BlockSpec(memory_space=pltpu.VMEM)
    return pl.pallas_call(
        place_body,
        out_shape=out,
        in_specs=[pl.BlockSpec(memory_space=pltpu.SMEM), *([vmem] * 4)],
        out_specs=vmem,
        compiler_params=pltpu.CompilerParams(vmem_limit_bytes=8 << 20),
        cost_estimate=cost(0, out, out),
        name="place",
    )(at, *parts)


def after(value, *others):
    return lax.optimization_barrier((value, *others))[0]


def by_x(k):
    return [(x, (x + k) % NX) for x in range(NX)]


def by_core(n, way, core_first):
    def index(k, c):
        return c * n + k % n if core_first else (k % n) * NC + c

    return [
        (index(k, c), index(k + way * (1 - 2 * c), c)) for k in range(n) for c in range(NC)
    ]


SWAP = [(0, 1), (1, 0)]


def local(activations, student_out, teacher_out, weight):
    x, zh, c, y = (lax.axis_index(n) for n in ("x", "zh", "core", "outc"))
    zl = lax.axis_index("inc")
    d = 1 - 2 * c
    own = weight[0]
    mb = activations.shape[0]

    def step_x(value, way=1):
        return lax.ppermute(value, ("x", "core"), by_core(NX, way, False))

    def step_y(value, way=1):
        return lax.ppermute(value, ("core", "outc"), by_core(NY, way, True))

    def swap_zh(value):
        return lax.ppermute(value, "zh", SWAP)

    def swap_core(value):
        return lax.ppermute(value, "core", SWAP)

    def neighbours(piece):
        return lax.ppermute(piece, "x", by_x(1)), lax.ppermute(piece, "x", by_x(-1))

    def pick(below, above):
        return jnp.where(c == 0, below, above)

    ways = (2, -d, d, 0)
    at_y = jnp.stack([(y + k) & (NY - 1) for k in ways])
    at_o = jnp.stack([*(((x + k) & (NX - 1)) * NZ + zh for k in ways), c])
    at_p = jnp.stack([*(((x + k) & (NX - 1)) * NZ + 1 - zh for k in ways), c])

    diff = (student_out.astype(F32) - teacher_out.astype(F32)).astype(BF16)
    diff_z = lax.ppermute(diff, "inc", SWAP)
    near_o = neighbours(own)
    w_z = swap_zh(own)
    act_send = other_columns(after(activations, *near_o), c)
    act_got = swap_core(act_send)
    w_o = (own, *near_o, step_x(pick(*near_o)))
    near_p = neighbours(w_z)
    w_p = (w_z, *near_p, step_x(pick(*near_p)))
    diff_z = after(diff_z, w_z, act_send, w_o[3])
    mine = jnp.where(
        zl == 0,
        jnp.concatenate([diff, diff_z], axis=1),
        jnp.concatenate([diff_z, diff], axis=1),
    )
    theirs = swap_core(mine)

    def add(*terms):
        total = terms[0].astype(F32)
        for t in terms[1:]:
            total = total + t.astype(F32)
        return total

    def ring(step, terms):
        far, back, ahead, here = terms
        far, back = step(far), step(back, -1)
        return add(here, back, step(add(ahead, far).astype(BF16)))

    terms = dx_terms(at_y, mine, theirs, w_o)
    theirs_w = after(theirs, *terms)
    dx_o = ring(step_y, terms).astype(BF16)
    terms_p = dw_terms(at_p, activations, act_got, mine, theirs_w)
    terms_o = dw_terms(at_o, activations, act_got, mine, after(theirs_w, *terms_p))
    cross = swap_zh(ring(step_x, terms_p).astype(BF16))
    weight_grad = ring(step_x, terms_o) + cross.astype(F32)
    dx_p = ring(step_y, dx_terms(at_y, mine, after(theirs, *terms_o), w_p)).astype(BF16)

    half = dx_o.shape[0] // 2
    got_o, got_p = swap_core(dx_o[half:]), swap_core(dx_p[half:])
    input_grad = place(
        jnp.stack([x, zh, c]), mb, dx_o[:half], got_o, dx_p[:half], got_p
    )
    return input_grad, weight_grad.reshape(weight.shape)


def solution(mesh):
    fine = Mesh(
        mesh.devices.reshape(NX, NZ, NC, NL, NY), ("x", "zh", "core", "inc", "outc")
    )
    tok = ("x", "zh", "core")
    placed = (
        P(None, tok, "inc"),
        P(None, (*tok, "inc"), "outc"),
        P(None, (*tok, "inc"), "outc"),
        P("inc", tok, "outc"),
    )
    return jax.shard_map(
        local,
        mesh=fine,
        in_specs=placed,
        out_specs=(P(None, (*tok, "outc"), "inc"), P("inc", tok, "outc")),
        check_vma=False,
    )
```

```python
import math

import jax
import jax.numpy as jnp
from jax import lax
from jax.experimental import pallas as pl
from jax.experimental.pallas import tpu as pltpu
from jax.sharding import Mesh
from jax.sharding import PartitionSpec as P

NX, NZ, NC, NL, NY = 4, 2, 2, 2, 4
F32, BF16 = jnp.float32, jnp.bfloat16
PIECES = (0, -1, 1, 2)


def cost(flops, *arrays):
    moved = sum(math.prod(a.shape) * jnp.dtype(a.dtype).itemsize for a in arrays)
    return pl.CostEstimate(flops=flops, bytes_accessed=moved, transcendentals=0)


HBM = pl.BlockSpec(memory_space=pltpu.HBM)
SMEM = pl.BlockSpec(memory_space=pltpu.SMEM)


def in_hbm(array):
    return pltpu.with_memory_space_constraint(array, pltpu.HBM)


def start_all(pairs, sems, first=0):
    copies = [
        pltpu.make_async_copy(src, dst, sems.at[first + k])
        for k, (src, dst) in enumerate(pairs)
    ]
    for copy in copies:
        copy.start()
    return copies


def wait_all(copies):
    for copy in copies:
        copy.wait()


def other_columns(act, c):
    mb, toks, width = act.shape
    n = NX * NZ
    rows = width // (n * NC)

    def body(core, act_ref, out_ref, sems):
        pairs = []
        for k in range(n):
            start = pl.multiple_of((k * NC + 1 - core[0]) * rows, rows)
            pairs.append((act_ref.at[:, :, pl.ds(start, rows)], out_ref.at[k]))
        wait_all(start_all(pairs, sems))

    out = pltpu.HBM((n, mb, toks, rows), act.dtype)
    return pl.pallas_call(
        body,
        out_shape=out,
        in_specs=[SMEM, HBM],
        out_specs=HBM,
        scratch_shapes=[pltpu.SemaphoreType.DMA((n,))],
        compiler_params=pltpu.CompilerParams(vmem_limit_bytes=1 << 20),
        cost_estimate=cost(0, out, out),
        name="other_columns",
    )(c.reshape(1), in_hbm(act))


def four_terms(rows, cols):
    return [pltpu.HBM((rows, cols), t) for t in (BF16, BF16, F32, F32)]


def dw_body(at, act, got, *refs):
    diffs, outs = refs[:4], refs[4:8]
    lhs, rhs, narrow, wide, sems = refs[8:]
    mb, part, cols = diffs[0].shape
    rows = got.shape[-1]
    toks = NL * part
    c, zl = at[4], at[5]
    loads = []
    for j, diff in enumerate(diffs):
        start = pl.multiple_of((zl if j % 2 == 0 else 1 - zl) * part, part)
        loads.append((diff, rhs.at[j // 2, :, pl.ds(start, part)]))
    for k in range(4):
        start = pl.multiple_of((at[k] * NC + c) * rows, rows)
        loads.append((act.at[:, :, pl.ds(start, rows)], lhs.at[k, 0]))
        loads.append((got.at[at[k]], lhs.at[k, 1]))
    loads = start_all(loads, sems)
    wait_all(loads[:4])
    stores = []
    step = cols // 2
    for k, out in enumerate(outs):
        wait_all(loads[4 + 2 * k : 6 + 2 * k])
        held = narrow.at[k] if k < 2 else wide.at[k - 2]
        for j in range(0, cols, step):
            total = None
            for n in range(NC):
                term = lax.dot_general(
                    lhs[k, n].reshape(mb * toks, rows),
                    rhs[n, :, :, j : j + step].reshape(mb * toks, step),
                    (((0,), (0,)), ((), ())),
                    preferred_element_type=F32,
                )
                total = term if total is None else total + term
            held[:, j : j + step] = total.astype(held.dtype)
        stores += start_all([(held, out)], sems, len(loads) + k)
    wait_all(stores)


def dw_terms(at, act, got, diffs):
    mb, part, cols = diffs[0].shape
    rows = got.shape[-1]
    toks = NL * part
    outs = four_terms(rows, cols)
    return pl.pallas_call(
        dw_body,
        out_shape=outs,
        in_specs=[SMEM, *([HBM] * 6)],
        out_specs=[HBM] * 4,
        scratch_shapes=[
            pltpu.VMEM((4, NC, mb, toks, rows), BF16),
            pltpu.VMEM((NC, mb, toks, cols), BF16),
            pltpu.VMEM((2, rows, cols), BF16),
            pltpu.VMEM((2, rows, cols), F32),
            pltpu.SemaphoreType.DMA((16,)),
        ],
        compiler_params=pltpu.CompilerParams(vmem_limit_bytes=20 << 20),
        cost_estimate=cost(16 * NC * mb * toks * rows * cols // 2, *outs, *diffs, got),
        name="dw_terms",
    )(at, in_hbm(act), got, *map(in_hbm, diffs))


def dx_body(at, *refs):
    diffs, pieces, outs = refs[:4], refs[4:8], refs[8:12]
    lhs, rhs, narrow, wide, sems = refs[12:]
    mb, toks, cols = diffs[0].shape
    part = toks // 2
    rows = pieces[0].shape[0]
    loads = [(piece, rhs.at[p]) for p, piece in enumerate(pieces)]
    for j, diff in enumerate(diffs):
        for h in range(2):
            k = at[j % 2 * 2 + h]
            for m in range(mb):
                src = diff.at[m, h * part : (h + 1) * part]
                loads.append((src, lhs.at[k, j // 2, m]))
    wait_all(start_all(loads, sems))
    each = NC * mb * part
    stores = []
    for g, held in enumerate((narrow, wide)):
        left = lhs[2 * g : 2 * g + 2].reshape(2 * each, cols)
        for p in range(NX):
            got = lax.dot_general(
                left, rhs[p], (((1,), (1,)), ((), ())), preferred_element_type=F32
            )
            for k in range(2):
                term = got[k * each : (k + 1) * each]
                held[k, :, p * rows : (p + 1) * rows] = term.astype(held.dtype)
        pairs = [(held.at[k], outs[2 * g + k]) for k in range(2)]
        stores += start_all(pairs, sems, len(loads) + 2 * g)
    wait_all(stores)


def dx_terms(at, diffs, pieces):
    mb, toks, cols = diffs[0].shape
    part = toks // 2
    rows = pieces[0].shape[0]
    outs = four_terms(NC * mb * part, NX * rows)
    return pl.pallas_call(
        dx_body,
        out_shape=outs,
        in_specs=[SMEM, *([HBM] * (4 + NX))],
        out_specs=[HBM] * 4,
        scratch_shapes=[
            pltpu.VMEM((4, NC, mb, part, cols), BF16),
            pltpu.VMEM((NX, rows, cols), BF16),
            pltpu.VMEM((2, NC * mb * part, NX * rows), BF16),
            pltpu.VMEM((2, NC * mb * part, NX * rows), F32),
            pltpu.SemaphoreType.DMA((NX + 16 + 4,)),
        ],
        compiler_params=pltpu.CompilerParams(vmem_limit_bytes=20 << 20),
        cost_estimate=cost(8 * math.prod(outs[0].shape) * cols, *outs, *diffs, *pieces),
        name="dx_terms",
    )(at, *map(in_hbm, (*diffs, *pieces)))


def place_body(at, keep_o, got_o, keep_p, got_p, out_ref):
    x, zh, c = at[0], at[1], at[2]
    mb, part, _ = out_ref.shape
    rows = keep_o.shape[-1] // NX
    for ref, z, n in (
        (keep_o, zh, c),
        (got_o, zh, 1 - c),
        (keep_p, 1 - zh, c),
        (got_p, 1 - zh, 1 - c),
    ):
        for p, away in enumerate(PIECES):
            start = ((((x + away) & (NX - 1)) * NZ + z) * NC + n) * rows
            lanes = pl.ds(pl.multiple_of(start, rows), rows)
            for m in range(mb):
                out_ref[m, :, lanes] = ref[
                    m * part : (m + 1) * part, p * rows : (p + 1) * rows
                ]


def place(at, mb, *parts):
    toks, width = parts[0].shape
    out = jax.ShapeDtypeStruct((mb, toks // mb, NZ * NC * width), BF16)
    vmem = pl.BlockSpec(memory_space=pltpu.VMEM)
    return pl.pallas_call(
        place_body,
        out_shape=out,
        in_specs=[pl.BlockSpec(memory_space=pltpu.SMEM), *([vmem] * 4)],
        out_specs=vmem,
        compiler_params=pltpu.CompilerParams(vmem_limit_bytes=8 << 20),
        cost_estimate=cost(0, out, out),
        name="place",
    )(at, *parts)


def after(value, *others):
    return lax.optimization_barrier((value, *others))[0]


def by_x(k):
    return [(x, (x + k) % NX) for x in range(NX)]


def by_core(n, way, core_first):
    def index(k, c):
        return c * n + k % n if core_first else (k % n) * NC + c

    return [
        (index(k, c), index(k + way * (1 - 2 * c), c)) for k in range(n) for c in range(NC)
    ]


SWAP = [(0, 1), (1, 0)]


def local(activations, student_out, teacher_out, weight):
    x, zh, c, y = (lax.axis_index(n) for n in ("x", "zh", "core", "outc"))
    zl = lax.axis_index("inc")
    d = 1 - 2 * c
    own = weight[0]
    mb = activations.shape[0]

    def step_x(value, way=1):
        return lax.ppermute(value, ("x", "core"), by_core(NX, way, False))

    def step_y(value, way=1):
        return lax.ppermute(value, ("core", "outc"), by_core(NY, way, True))

    def swap_zh(value):
        return lax.ppermute(value, "zh", SWAP)

    def swap_core(value):
        return lax.ppermute(value, "core", SWAP)

    def neighbours(piece):
        return lax.ppermute(piece, "x", by_x(1)), lax.ppermute(piece, "x", by_x(-1))

    def pick(below, above):
        return jnp.where(c == 0, below, above)

    ways = (2, -d, d, 0)
    at_o = jnp.stack([*(((x + k) & (NX - 1)) * NZ + zh for k in ways), c, zl])
    at_p = jnp.stack([*(((x + k) & (NX - 1)) * NZ + 1 - zh for k in ways), c, zl])

    def place_of(z, h):
        away = (2 * z + h - y) & (NY - 1)
        beside = jnp.where(away == (d & (NY - 1)), 2, 1)
        return jnp.where(away == 2, 0, jnp.where(away == 0, 3, beside))

    at_y = jnp.stack([place_of(z, h) for z in (zl, 1 - zl) for h in range(2)])

    act_send = other_columns(activations, c)
    student_out = after(student_out, act_send)
    diff = (student_out.astype(F32) - teacher_out.astype(F32)).astype(BF16)
    diff_z = lax.ppermute(diff, "inc", SWAP)
    near_o = neighbours(own)
    w_z = swap_zh(own)
    act_got = swap_core(act_send)
    diff_c = swap_core(diff)
    w_o = (own, *near_o, step_x(pick(*near_o)))
    near_p = neighbours(w_z)
    diff_z = after(diff_z, w_z)
    diffs = (diff, diff_z, diff_c, swap_core(diff_z))

    def later(*others):
        return (after(diff, *others), *diffs[1:])

    def add(*terms):
        total = terms[0].astype(F32)
        for t in terms[1:]:
            total = total + t.astype(F32)
        return total

    def ring(step, terms, *first):
        far, back, ahead, here = terms
        far, back = after(step(far), *first), step(back, -1)
        return add(here, back, step(add(ahead, far).astype(BF16)))

    terms = dx_terms(at_y, diffs, w_o)
    terms_p = dw_terms(at_p, activations, act_got, later(*terms))
    terms_o = dw_terms(at_o, activations, act_got, later(*terms_p))
    far_p = step_x(pick(after(near_p[0], terms_p[0]), near_p[1]))
    w_p = (w_z, *near_p, far_p)
    dx_o = ring(step_y, terms, terms_p[0]).astype(BF16)
    cross = swap_zh(ring(step_x, terms_p).astype(BF16))
    weight_grad = ring(step_x, terms_o) + cross.astype(F32)
    dx_p = ring(step_y, dx_terms(at_y, later(*terms_o), w_p)).astype(BF16)

    half = dx_o.shape[0] // 2
    got_o, got_p = swap_core(dx_o[half:]), swap_core(dx_p[half:])
    input_grad = place(
        jnp.stack([x, zh, c]), mb, dx_o[:half], got_o, dx_p[:half], got_p
    )
    return input_grad, weight_grad.reshape(weight.shape)


def solution(mesh):
    fine = Mesh(
        mesh.devices.reshape(NX, NZ, NC, NL, NY), ("x", "zh", "core", "inc", "outc")
    )
    tok = ("x", "zh", "core")
    placed = (
        P(None, tok, "inc"),
        P(None, (*tok, "inc"), "outc"),
        P(None, (*tok, "inc"), "outc"),
        P("inc", tok, "outc"),
    )
    return jax.shard_map(
        local,
        mesh=fine,
        in_specs=placed,
        out_specs=(P(None, (*tok, "outc"), "inc"), P("inc", tok, "outc")),
        check_vma=False,
    )
```

```python
import math

import jax
import jax.numpy as jnp
from jax import lax
from jax.experimental import pallas as pl
from jax.experimental.pallas import tpu as pltpu
from jax.sharding import Mesh
from jax.sharding import PartitionSpec as P

NX, NZ, NC, NL, NY = 4, 2, 2, 2, 4
F32, BF16 = jnp.float32, jnp.bfloat16
PIECES = (0, -1, 1, 2)


def cost(flops, *arrays):
    moved = sum(math.prod(a.shape) * jnp.dtype(a.dtype).itemsize for a in arrays)
    return pl.CostEstimate(flops=flops, bytes_accessed=moved, transcendentals=0)


HBM = pl.BlockSpec(memory_space=pltpu.HBM)
SMEM = pl.BlockSpec(memory_space=pltpu.SMEM)


def in_hbm(array):
    return pltpu.with_memory_space_constraint(array, pltpu.HBM)


def start_all(pairs, sems, first=0):
    copies = [
        pltpu.make_async_copy(src, dst, sems.at[first + k])
        for k, (src, dst) in enumerate(pairs)
    ]
    for copy in copies:
        copy.start()
    return copies


def wait_all(copies):
    for copy in copies:
        copy.wait()


def other_columns(act, c):
    mb, toks, width = act.shape
    n = NX * NZ
    rows = width // (n * NC)

    def body(core, act_ref, out_ref):
        pick = core[0] == 0
        out_ref[0] = jnp.where(pick, act_ref[:, :, rows:], act_ref[:, :, :rows])

    out = pltpu.HBM((n, mb, toks, rows), act.dtype)
    return pl.pallas_call(
        body,
        out_shape=out,
        grid=(n,),
        in_specs=[SMEM, pl.BlockSpec((mb, toks, NC * rows), lambda k: (0, 0, k))],
        out_specs=pl.BlockSpec((1, mb, toks, rows), lambda k: (k, 0, 0, 0)),
        compiler_params=pltpu.CompilerParams(vmem_limit_bytes=8 << 20),
        cost_estimate=cost(0, act, out),
        name="other_columns",
    )(c.reshape(1), in_hbm(act))


def four_terms(rows, cols):
    return [pltpu.HBM((rows, cols), t) for t in (BF16, BF16, F32, F32)]


def dw_body(at, act, got, *refs):
    diffs, outs = refs[:4], refs[4:8]
    lhs, rhs, narrow, wide, sems = refs[8:]
    mb, part, cols = diffs[0].shape
    rows = got.shape[-1]
    toks = NL * part
    c, zl = at[4], at[5]
    loads = []
    for j, diff in enumerate(diffs):
        start = pl.multiple_of((zl if j % 2 == 0 else 1 - zl) * part, part)
        loads.append((diff, rhs.at[j // 2, :, pl.ds(start, part)]))
    for k in range(4):
        start = pl.multiple_of((at[k] * NC + c) * rows, rows)
        loads.append((act.at[:, :, pl.ds(start, rows)], lhs.at[k, 0]))
        loads.append((got.at[at[k]], lhs.at[k, 1]))
    loads = start_all(loads, sems)
    wait_all(loads[:4])
    stores = []
    step = cols // 2
    for k, out in enumerate(outs):
        wait_all(loads[4 + 2 * k : 6 + 2 * k])
        held = narrow.at[k] if k < 2 else wide.at[k - 2]
        for j in range(0, cols, step):
            total = None
            for n in range(NC):
                term = lax.dot_general(
                    lhs[k, n].reshape(mb * toks, rows),
                    rhs[n, :, :, j : j + step].reshape(mb * toks, step),
                    (((0,), (0,)), ((), ())),
                    preferred_element_type=F32,
                )
                total = term if total is None else total + term
            held[:, j : j + step] = total.astype(held.dtype)
        stores += start_all([(held, out)], sems, len(loads) + k)
    wait_all(stores)


def dw_terms(at, act, got, diffs):
    mb, part, cols = diffs[0].shape
    rows = got.shape[-1]
    toks = NL * part
    outs = four_terms(rows, cols)
    return pl.pallas_call(
        dw_body,
        out_shape=outs,
        in_specs=[SMEM, *([HBM] * 6)],
        out_specs=[HBM] * 4,
        scratch_shapes=[
            pltpu.VMEM((4, NC, mb, toks, rows), BF16),
            pltpu.VMEM((NC, mb, toks, cols), BF16),
            pltpu.VMEM((2, rows, cols), BF16),
            pltpu.VMEM((2, rows, cols), F32),
            pltpu.SemaphoreType.DMA((16,)),
        ],
        compiler_params=pltpu.CompilerParams(vmem_limit_bytes=20 << 20),
        cost_estimate=cost(16 * NC * mb * toks * rows * cols // 2, *outs, *diffs, got),
        name="dw_terms",
    )(at, in_hbm(act), got, *diffs)


def dx_body(at, *refs):
    diffs, pieces, outs = refs[:4], refs[4:8], refs[8:12]
    lhs, rhs, narrow, wide, sems = refs[12:]
    mb, toks, cols = diffs[0].shape
    part = toks // 2
    rows = pieces[0].shape[0]
    loads = [(piece, rhs.at[p]) for p, piece in enumerate(pieces)]
    for j, diff in enumerate(diffs):
        for h in range(2):
            k = at[j % 2 * 2 + h]
            for m in range(mb):
                src = diff.at[m, h * part : (h + 1) * part]
                loads.append((src, lhs.at[k, j // 2, m]))
    wait_all(start_all(loads, sems))
    each = NC * mb * part
    stores = []
    for g, held in enumerate((narrow, wide)):
        left = lhs[2 * g : 2 * g + 2].reshape(2 * each, cols)
        for p in range(NX):
            got = lax.dot_general(
                left, rhs[p], (((1,), (1,)), ((), ())), preferred_element_type=F32
            )
            for k in range(2):
                term = got[k * each : (k + 1) * each]
                held[k, :, p * rows : (p + 1) * rows] = term.astype(held.dtype)
        pairs = [(held.at[k], outs[2 * g + k]) for k in range(2)]
        stores += start_all(pairs, sems, len(loads) + 2 * g)
    wait_all(stores)


def dx_terms(at, diffs, pieces):
    mb, toks, cols = diffs[0].shape
    part = toks // 2
    rows = pieces[0].shape[0]
    outs = four_terms(NC * mb * part, NX * rows)
    return pl.pallas_call(
        dx_body,
        out_shape=outs,
        in_specs=[SMEM, *([HBM] * (4 + NX))],
        out_specs=[HBM] * 4,
        scratch_shapes=[
            pltpu.VMEM((4, NC, mb, part, cols), BF16),
            pltpu.VMEM((NX, rows, cols), BF16),
            pltpu.VMEM((2, NC * mb * part, NX * rows), BF16),
            pltpu.VMEM((2, NC * mb * part, NX * rows), F32),
            pltpu.SemaphoreType.DMA((NX + 16 + 4,)),
        ],
        compiler_params=pltpu.CompilerParams(vmem_limit_bytes=20 << 20),
        cost_estimate=cost(8 * math.prod(outs[0].shape) * cols, *outs, *diffs, *pieces),
        name="dx_terms",
    )(at, *diffs, *map(in_hbm, pieces))


def place_body(at, keep_o, got_o, keep_p, got_p, out_ref):
    x, zh, c = at[0], at[1], at[2]
    mb, part, _ = out_ref.shape
    rows = keep_o.shape[-1] // NX
    for ref, z, n in (
        (keep_o, zh, c),
        (got_o, zh, 1 - c),
        (keep_p, 1 - zh, c),
        (got_p, 1 - zh, 1 - c),
    ):
        for p, away in enumerate(PIECES):
            start = ((((x + away) & (NX - 1)) * NZ + z) * NC + n) * rows
            lanes = pl.ds(pl.multiple_of(start, rows), rows)
            for m in range(mb):
                out_ref[m, :, lanes] = ref[
                    m * part : (m + 1) * part, p * rows : (p + 1) * rows
                ]


def place(at, mb, *parts):
    toks, width = parts[0].shape
    out = jax.ShapeDtypeStruct((mb, toks // mb, NZ * NC * width), BF16)
    vmem = pl.BlockSpec(memory_space=pltpu.VMEM)
    return pl.pallas_call(
        place_body,
        out_shape=out,
        in_specs=[pl.BlockSpec(memory_space=pltpu.SMEM), *([vmem] * 4)],
        out_specs=vmem,
        compiler_params=pltpu.CompilerParams(vmem_limit_bytes=8 << 20),
        cost_estimate=cost(0, out, out),
        name="place",
    )(at, *parts)


def after(value, *others):
    return lax.optimization_barrier((value, *others))[0]


def by_x(k):
    return [(x, (x + k) % NX) for x in range(NX)]


def by_core(n, way, core_first):
    def index(k, c):
        return c * n + k % n if core_first else (k % n) * NC + c

    return [
        (index(k, c), index(k + way * (1 - 2 * c), c)) for k in range(n) for c in range(NC)
    ]


SWAP = [(0, 1), (1, 0)]


def local(activations, student_out, teacher_out, weight):
    x, zh, c, y = (lax.axis_index(n) for n in ("x", "zh", "core", "outc"))
    zl = lax.axis_index("inc")
    d = 1 - 2 * c
    own = weight[0]
    mb = activations.shape[0]

    def step_x(value, way=1):
        return lax.ppermute(value, ("x", "core"), by_core(NX, way, False))

    def step_y(value, way=1):
        return lax.ppermute(value, ("core", "outc"), by_core(NY, way, True))

    def swap_zh(value):
        return lax.ppermute(value, "zh", SWAP)

    def swap_core(value):
        return lax.ppermute(value, "core", SWAP)

    def neighbours(piece):
        return lax.ppermute(piece, "x", by_x(1)), lax.ppermute(piece, "x", by_x(-1))

    def pick(below, above):
        return jnp.where(c == 0, below, above)

    ways = (2, -d, d, 0)
    at_o = jnp.stack([*(((x + k) & (NX - 1)) * NZ + zh for k in ways), c, zl])
    at_p = jnp.stack([*(((x + k) & (NX - 1)) * NZ + 1 - zh for k in ways), c, zl])

    def place_of(z, h):
        away = (2 * z + h - y) & (NY - 1)
        beside = jnp.where(away == (d & (NY - 1)), 2, 1)
        return jnp.where(away == 2, 0, jnp.where(away == 0, 3, beside))

    at_y = jnp.stack([place_of(z, h) for z in (zl, 1 - zl) for h in range(2)])

    diff = (student_out.astype(F32) - teacher_out.astype(F32)).astype(BF16)
    diff_z = lax.ppermute(diff, "inc", SWAP)
    own_late = after(own, diff)
    near_o = neighbours(own_late)
    w_z = swap_zh(own_late)
    diff_c = swap_core(diff)
    near_p = neighbours(w_z)
    far_o = step_x(pick(*near_o))
    diff_z = after(diff_z, w_z, diff_c, far_o)
    act_got = swap_core(other_columns(after(activations, diff_z), c))
    diffs = (diff, diff_z, diff_c, swap_core(diff_z))

    def later(*others):
        return (after(diff, *others), *diffs[1:])

    def add(*terms):
        total = terms[0].astype(F32)
        for t in terms[1:]:
            total = total + t.astype(F32)
        return total

    def ring(step, terms, *first):
        far, back, ahead, here = terms
        far, back = lax.optimization_barrier((step(far), step(back, -1), *first))[:2]
        return add(here, back, step(add(ahead, far).astype(BF16)))

    terms_o = dx_terms(at_y, diffs, (own, *near_o, far_o))
    forward_p = pick(after(near_p[0], terms_o[0]), near_p[1])
    sums_p = dw_terms(at_p, activations, act_got, later(forward_p))
    w_p = (w_z, *near_p, step_x(forward_p))
    terms_p = dx_terms(at_y, later(*sums_p), w_p)
    sums_o = dw_terms(at_o, activations, act_got, later(*terms_p))
    dx_o = ring(step_y, terms_o, sums_p[0]).astype(BF16)
    cross = swap_zh(ring(step_x, sums_p).astype(BF16))
    dx_p = ring(step_y, terms_p).astype(BF16)
    weight_grad = ring(step_x, sums_o) + cross.astype(F32)

    half = dx_o.shape[0] // 2
    got_o, got_p = swap_core(dx_o[half:]), swap_core(dx_p[half:])
    input_grad = place(
        jnp.stack([x, zh, c]), mb, dx_o[:half], got_o, dx_p[:half], got_p
    )
    return input_grad, weight_grad.reshape(weight.shape)


def solution(mesh):
    fine = Mesh(
        mesh.devices.reshape(NX, NZ, NC, NL, NY), ("x", "zh", "core", "inc", "outc")
    )
    tok = ("x", "zh", "core")
    placed = (
        P(None, tok, "inc"),
        P(None, (*tok, "inc"), "outc"),
        P(None, (*tok, "inc"), "outc"),
        P("inc", tok, "outc"),
    )
    return jax.shard_map(
        local,
        mesh=fine,
        in_specs=placed,
        out_specs=(P(None, (*tok, "outc"), "inc"), P("inc", tok, "outc")),
        check_vma=False,
    )
```

```python
import math

import jax
import jax.numpy as jnp
from jax import lax
from jax.experimental import pallas as pl
from jax.experimental.pallas import tpu as pltpu
from jax.sharding import Mesh
from jax.sharding import PartitionSpec as P

NX, NZ, NC, NL, NY = 4, 2, 2, 2, 4
F32, BF16 = jnp.float32, jnp.bfloat16
PIECES = (0, -1, 1, 2)


def cost(flops, *arrays):
    moved = sum(math.prod(a.shape) * jnp.dtype(a.dtype).itemsize for a in arrays)
    return pl.CostEstimate(flops=flops, bytes_accessed=moved, transcendentals=0)


HBM = pl.BlockSpec(memory_space=pltpu.HBM)
SMEM = pl.BlockSpec(memory_space=pltpu.SMEM)


def in_hbm(array):
    return pltpu.with_memory_space_constraint(array, pltpu.HBM)


def start_all(pairs, sems, first=0):
    copies = [
        pltpu.make_async_copy(src, dst, sems.at[first + k])
        for k, (src, dst) in enumerate(pairs)
    ]
    for copy in copies:
        copy.start()
    return copies


def wait_all(copies):
    for copy in copies:
        copy.wait()


def other_columns(act, c):
    mb, toks, width = act.shape
    n = NX * NZ
    rows = width // (n * NC)

    def body(core, act_ref, out_ref, held, sems):
        loads = []
        for k in range(n):
            start = pl.multiple_of((k * NC + 1 - core[0]) * rows, rows)
            loads.append((act_ref.at[:, :, pl.ds(start, rows)], held.at[k]))
        stores = []
        for k, load in enumerate(start_all(loads, sems)):
            load.wait()
            stores += start_all([(held.at[k], out_ref.at[k])], sems, n + k)
        wait_all(stores)

    out = pltpu.HBM((n, mb, toks, rows), act.dtype)
    return pl.pallas_call(
        body,
        out_shape=out,
        in_specs=[SMEM, HBM],
        out_specs=HBM,
        scratch_shapes=[
            pltpu.VMEM((n, mb, toks, rows), act.dtype),
            pltpu.SemaphoreType.DMA((2 * n,)),
        ],
        compiler_params=pltpu.CompilerParams(vmem_limit_bytes=4 << 20),
        cost_estimate=cost(0, act, out),
        name="other_columns",
    )(c.reshape(1), in_hbm(act))


def four_terms(rows, cols):
    return [pltpu.HBM((rows, cols), t) for t in (BF16, BF16, F32, F32)]


def dw_body(at, act, got, *refs):
    diffs, outs = refs[:4], refs[4:8]
    lhs, rhs, narrow, wide, sems = refs[8:]
    mb, part, cols = diffs[0].shape
    rows = got.shape[-1]
    toks = NL * part
    c, zl = at[4], at[5]
    loads = []
    for j, diff in enumerate(diffs):
        start = pl.multiple_of((zl if j % 2 == 0 else 1 - zl) * part, part)
        loads.append((diff, rhs.at[j // 2, :, pl.ds(start, part)]))
    for k in range(4):
        start = pl.multiple_of((at[k] * NC + c) * rows, rows)
        loads.append((act.at[:, :, pl.ds(start, rows)], lhs.at[k, 0]))
        loads.append((got.at[at[k]], lhs.at[k, 1]))
    loads = start_all(loads, sems)
    wait_all(loads[:4])
    stores = []
    step = cols // 2
    for k, out in enumerate(outs):
        wait_all(loads[4 + 2 * k : 6 + 2 * k])
        held = narrow.at[k] if k < 2 else wide.at[k - 2]
        for j in range(0, cols, step):
            total = None
            for n in range(NC):
                term = lax.dot_general(
                    lhs[k, n].reshape(mb * toks, rows),
                    rhs[n, :, :, j : j + step].reshape(mb * toks, step),
                    (((0,), (0,)), ((), ())),
                    preferred_element_type=F32,
                )
                total = term if total is None else total + term
            held[:, j : j + step] = total.astype(held.dtype)
        stores += start_all([(held, out)], sems, len(loads) + k)
    wait_all(stores)


def dw_terms(at, act, got, diffs):
    mb, part, cols = diffs[0].shape
    rows = got.shape[-1]
    toks = NL * part
    outs = four_terms(rows, cols)
    return pl.pallas_call(
        dw_body,
        out_shape=outs,
        in_specs=[SMEM, *([HBM] * 6)],
        out_specs=[HBM] * 4,
        scratch_shapes=[
            pltpu.VMEM((4, NC, mb, toks, rows), BF16),
            pltpu.VMEM((NC, mb, toks, cols), BF16),
            pltpu.VMEM((2, rows, cols), BF16),
            pltpu.VMEM((2, rows, cols), F32),
            pltpu.SemaphoreType.DMA((16,)),
        ],
        compiler_params=pltpu.CompilerParams(vmem_limit_bytes=16 << 20),
        cost_estimate=cost(8 * NC * mb * toks * rows * cols, *outs, *diffs, got),
        name="dw_terms",
    )(at, *map(in_hbm, (act, got, *diffs)))


def dx_body(at, *refs):
    diffs, pieces, outs = refs[:4], refs[4:8], refs[8:12]
    lhs, rhs, narrow, wide, sems = refs[12:]
    mb, toks, cols = diffs[0].shape
    part = toks // 2
    rows = pieces[0].shape[0]
    loads = []
    for j, diff in enumerate(diffs):
        for h in range(2):
            k = at[j % 2 * 2 + h]
            for m in range(mb):
                src = diff.at[m, h * part : (h + 1) * part]
                loads.append((src, lhs.at[k, j // 2, m]))
    first = len(loads)
    loads += [(piece, rhs.at[p]) for p, piece in enumerate(pieces)]
    loads = start_all(loads, sems)
    wait_all(loads[:first])
    each = NC * mb * part
    left = lhs[...].reshape(4 * each, cols)
    stores = []
    for p in range(NX):
        loads[first + p].wait()
        got = lax.dot_general(
            left, rhs[p], (((1,), (1,)), ((), ())), preferred_element_type=F32
        )
        pairs = []
        for k, out in enumerate(outs):
            held = narrow if k < 2 else wide
            at_p = slice(p * rows, (p + 1) * rows)
            term = got[k * each : (k + 1) * each]
            held[k % 2, :, at_p] = term.astype(held.dtype)
            pairs.append((held.at[k % 2, :, at_p], out.at[:, at_p]))
        stores += start_all(pairs, sems, len(loads) + 4 * p)
    wait_all(stores)


def dx_terms(at, diffs, pieces):
    mb, toks, cols = diffs[0].shape
    part = toks // 2
    rows = pieces[0].shape[0]
    outs = four_terms(NC * mb * part, NX * rows)
    return pl.pallas_call(
        dx_body,
        out_shape=outs,
        in_specs=[SMEM, *([HBM] * (4 + NX))],
        out_specs=[HBM] * 4,
        scratch_shapes=[
            pltpu.VMEM((4, NC, mb, part, cols), BF16),
            pltpu.VMEM((NX, rows, cols), BF16),
            pltpu.VMEM((2, NC * mb * part, NX * rows), BF16),
            pltpu.VMEM((2, NC * mb * part, NX * rows), F32),
            pltpu.SemaphoreType.DMA((8 * mb + 5 * NX,)),
        ],
        compiler_params=pltpu.CompilerParams(vmem_limit_bytes=16 << 20),
        cost_estimate=cost(8 * math.prod(outs[0].shape) * cols, *outs, *diffs, *pieces),
        name="dx_terms",
    )(at, *map(in_hbm, (*diffs, *pieces)))


def place_body(at, keep_o, got_o, keep_p, got_p, out_ref):
    x, zh, c = at[0], at[1], at[2]
    mb, part, _ = out_ref.shape
    rows = keep_o.shape[-1] // NX
    for ref, z, n in (
        (keep_o, zh, c),
        (got_o, zh, 1 - c),
        (keep_p, 1 - zh, c),
        (got_p, 1 - zh, 1 - c),
    ):
        for p, away in enumerate(PIECES):
            start = ((((x + away) & (NX - 1)) * NZ + z) * NC + n) * rows
            lanes = pl.ds(pl.multiple_of(start, rows), rows)
            for m in range(mb):
                out_ref[m, :, lanes] = ref[
                    m * part : (m + 1) * part, p * rows : (p + 1) * rows
                ]


def place(at, mb, *parts):
    toks, width = parts[0].shape
    out = jax.ShapeDtypeStruct((mb, toks // mb, NZ * NC * width), BF16)
    vmem = pl.BlockSpec(memory_space=pltpu.VMEM)
    return pl.pallas_call(
        place_body,
        out_shape=out,
        in_specs=[pl.BlockSpec(memory_space=pltpu.SMEM), *([vmem] * 4)],
        out_specs=vmem,
        compiler_params=pltpu.CompilerParams(vmem_limit_bytes=8 << 20),
        cost_estimate=cost(0, out, out),
        name="place",
    )(at, *parts)


def after(value, *others):
    return lax.optimization_barrier((value, *others))[0]


def by_x(k):
    return [(x, (x + k) % NX) for x in range(NX)]


def by_core(n, way, core_first):
    def index(k, c):
        return c * n + k % n if core_first else (k % n) * NC + c

    return [
        (index(k, c), index(k + way * (1 - 2 * c), c)) for k in range(n) for c in range(NC)
    ]


SWAP = [(0, 1), (1, 0)]


def local(activations, student_out, teacher_out, weight):
    x, zh, c, y = (lax.axis_index(n) for n in ("x", "zh", "core", "outc"))
    zl = lax.axis_index("inc")
    d = 1 - 2 * c
    own = weight[0]
    mb = activations.shape[0]

    def step_x(value, way=1):
        return lax.ppermute(value, ("x", "core"), by_core(NX, way, False))

    def step_y(value, way=1):
        return lax.ppermute(value, ("core", "outc"), by_core(NY, way, True))

    def swap_zh(value):
        return lax.ppermute(value, "zh", SWAP)

    def swap_core(value):
        return lax.ppermute(value, "core", SWAP)

    def neighbours(piece):
        return lax.ppermute(piece, "x", by_x(1)), lax.ppermute(piece, "x", by_x(-1))

    def pick(below, above):
        return jnp.where(c == 0, below, above)

    ways = (2, -d, d, 0)
    at_o = jnp.stack([*(((x + k) & (NX - 1)) * NZ + zh for k in ways), c, zl])
    at_p = jnp.stack([*(((x + k) & (NX - 1)) * NZ + 1 - zh for k in ways), c, zl])

    def place_of(z, h):
        away = (2 * z + h - y) & (NY - 1)
        beside = jnp.where(away == (d & (NY - 1)), 2, 1)
        return jnp.where(away == 2, 0, jnp.where(away == 0, 3, beside))

    at_y = jnp.stack([place_of(z, h) for z in (zl, 1 - zl) for h in range(2)])

    diff = (student_out.astype(F32) - teacher_out.astype(F32)).astype(BF16)
    diff_z = lax.ppermute(diff, "inc", SWAP)
    diff_c = swap_core(diff)
    near_o = neighbours(after(own, diff))
    far_o = step_x(pick(*near_o))
    w_z = swap_zh(after(own, diff_z))
    diff_z = after(diff_z, diff_c, *near_o)
    diffs = (diff, diff_z, diff_c, swap_core(diff_z))
    act_got = swap_core(other_columns(after(activations, diff_z), c))

    def later(*others):
        return (after(diff, *others), *diffs[1:])

    def add(*terms):
        total = terms[0].astype(F32)
        for t in terms[1:]:
            total = total + t.astype(F32)
        return total

    def ring(step, terms, *first):
        far, back, ahead, here = terms
        far, back = lax.optimization_barrier((step(far), step(back, -1), *first))[:2]
        return add(here, back, step(add(ahead, far).astype(BF16)))

    terms_o = dx_terms(at_y, diffs, (own, *near_o, far_o))
    near_p = neighbours(after(w_z, terms_o[0]))
    sums_p = dw_terms(at_p, activations, act_got, later(*terms_o))
    forward_p = pick(after(near_p[0], sums_p[0]), near_p[1])
    sums_o = dw_terms(at_o, activations, act_got, later(forward_p))
    terms_p = dx_terms(at_y, later(*sums_o), (w_z, *near_p, step_x(forward_p)))
    dx_o = ring(step_y, terms_o, sums_p[0]).astype(BF16)
    cross = swap_zh(ring(step_x, sums_p).astype(BF16))
    weight_grad = ring(step_x, sums_o) + cross.astype(F32)
    dx_p = ring(step_y, terms_p).astype(BF16)

    half = dx_o.shape[0] // 2
    got_o, got_p = swap_core(dx_o[half:]), swap_core(dx_p[half:])
    input_grad = place(
        jnp.stack([x, zh, c]), mb, dx_o[:half], got_o, dx_p[:half], got_p
    )
    return input_grad, weight_grad.reshape(weight.shape)


def solution(mesh):
    fine = Mesh(
        mesh.devices.reshape(NX, NZ, NC, NL, NY), ("x", "zh", "core", "inc", "outc")
    )
    tok = ("x", "zh", "core")
    placed = (
        P(None, tok, "inc"),
        P(None, (*tok, "inc"), "outc"),
        P(None, (*tok, "inc"), "outc"),
        P("inc", tok, "outc"),
    )
    return jax.shard_map(
        local,
        mesh=fine,
        in_specs=placed,
        out_specs=(P(None, (*tok, "outc"), "inc"), P("inc", tok, "outc")),
        check_vma=False,
    )
```

```python
import math

import jax
import jax.numpy as jnp
from jax import lax
from jax.experimental import pallas as pl
from jax.experimental.pallas import tpu as pltpu
from jax.sharding import Mesh
from jax.sharding import PartitionSpec as P

NX, NZ, NC, NL, NY = 4, 2, 2, 2, 4
F32, BF16 = jnp.float32, jnp.bfloat16
PIECES = (0, -1, 1, 2)


def cost(flops, *arrays):
    moved = sum(math.prod(a.shape) * jnp.dtype(a.dtype).itemsize for a in arrays)
    return pl.CostEstimate(flops=flops, bytes_accessed=moved, transcendentals=0)


HBM = pl.BlockSpec(memory_space=pltpu.HBM)
SMEM = pl.BlockSpec(memory_space=pltpu.SMEM)


def in_hbm(array):
    return pltpu.with_memory_space_constraint(array, pltpu.HBM)


def start_all(pairs, sems, first=0):
    copies = [
        pltpu.make_async_copy(src, dst, sems.at[first + k])
        for k, (src, dst) in enumerate(pairs)
    ]
    for copy in copies:
        copy.start()
    return copies


def wait_all(copies):
    for copy in copies:
        copy.wait()


def other_columns(act, c):
    mb, toks, width = act.shape
    n = NX * NZ
    rows = width // (n * NC)

    def body(core, act_ref, out_ref, held, sems):
        loads = []
        for k in range(n):
            start = pl.multiple_of((k * NC + 1 - core[0]) * rows, rows)
            loads.append((act_ref.at[:, :, pl.ds(start, rows)], held.at[k]))
        stores = []
        for k, load in enumerate(start_all(loads, sems)):
            load.wait()
            stores += start_all([(held.at[k], out_ref.at[k])], sems, n + k)
        wait_all(stores)

    out = pltpu.HBM((n, mb, toks, rows), act.dtype)
    return pl.pallas_call(
        body,
        out_shape=out,
        in_specs=[SMEM, HBM],
        out_specs=HBM,
        scratch_shapes=[
            pltpu.VMEM((n, mb, toks, rows), act.dtype),
            pltpu.SemaphoreType.DMA((2 * n,)),
        ],
        compiler_params=pltpu.CompilerParams(vmem_limit_bytes=4 << 20),
        cost_estimate=cost(0, act, out),
        name="other_columns",
    )(c.reshape(1), in_hbm(act))


def four_terms(rows, cols):
    return [pltpu.HBM((rows, cols), t) for t in (BF16, BF16, F32, F32)]


def dw_body(at, act, got, *refs):
    diffs, outs = refs[:4], refs[4:8]
    lhs, rhs, narrow, wide, sems = refs[8:]
    mb, part, cols = diffs[0].shape
    rows = got.shape[-1]
    toks = NL * part
    c, zl = at[4], at[5]
    loads = []
    for j, diff in enumerate(diffs):
        start = pl.multiple_of((zl if j % 2 == 0 else 1 - zl) * part, part)
        loads.append((diff, rhs.at[j // 2, :, pl.ds(start, part)]))
    for k in range(4):
        start = pl.multiple_of((at[k] * NC + c) * rows, rows)
        loads.append((act.at[:, :, pl.ds(start, rows)], lhs.at[k, 0]))
        loads.append((got.at[at[k]], lhs.at[k, 1]))
    loads = start_all(loads, sems)
    wait_all(loads[:4])
    stores = []
    step = cols // 2
    for k, out in enumerate(outs):
        wait_all(loads[4 + 2 * k : 6 + 2 * k])
        held = narrow.at[k] if k < 2 else wide.at[k - 2]
        for j in range(0, cols, step):
            total = None
            for n in range(NC):
                term = lax.dot_general(
                    lhs[k, n].reshape(mb * toks, rows),
                    rhs[n, :, :, j : j + step].reshape(mb * toks, step),
                    (((0,), (0,)), ((), ())),
                    preferred_element_type=F32,
                )
                total = term if total is None else total + term
            held[:, j : j + step] = total.astype(held.dtype)
        stores += start_all([(held, out)], sems, len(loads) + k)
    wait_all(stores)


def dw_terms(at, act, got, diffs):
    mb, part, cols = diffs[0].shape
    rows = got.shape[-1]
    toks = NL * part
    outs = four_terms(rows, cols)
    return pl.pallas_call(
        dw_body,
        out_shape=outs,
        in_specs=[SMEM, *([HBM] * 6)],
        out_specs=[HBM] * 4,
        scratch_shapes=[
            pltpu.VMEM((4, NC, mb, toks, rows), BF16),
            pltpu.VMEM((NC, mb, toks, cols), BF16),
            pltpu.VMEM((2, rows, cols), BF16),
            pltpu.VMEM((2, rows, cols), F32),
            pltpu.SemaphoreType.DMA((16,)),
        ],
        compiler_params=pltpu.CompilerParams(vmem_limit_bytes=16 << 20),
        cost_estimate=cost(8 * NC * mb * toks * rows * cols, *outs, *diffs, got),
        name="dw_terms",
    )(at, in_hbm(act), got, *map(in_hbm, diffs))


def dx_body(at, *refs):
    diffs, pieces, outs = refs[:4], refs[4:8], refs[8:12]
    held, lhs, rhs, narrow, wide, sems = refs[12:]
    mb, toks, cols = diffs[0].shape
    part = toks // 2
    rows = pieces[0].shape[0]
    loads = [(diff, held.at[j]) for j, diff in enumerate(diffs)]
    loads += [(piece, rhs.at[p]) for p, piece in enumerate(pieces)]
    loads = start_all(loads, sems)
    for j in range(4):
        loads[j].wait()
        for h in range(2):
            k = at[j % 2 * 2 + h]
            for m in range(mb):
                lhs[k, j // 2, m] = held[j, m, h * part : (h + 1) * part]
    wait_all(loads[4:])
    each = NC * mb * part
    stores = []
    for g, terms in enumerate((narrow, wide)):
        left = lhs[2 * g : 2 * g + 2].reshape(2 * each, cols)
        for p in range(NX):
            got = lax.dot_general(
                left, rhs[p], (((1,), (1,)), ((), ())), preferred_element_type=F32
            )
            for k in range(2):
                term = got[k * each : (k + 1) * each]
                terms[k, :, p * rows : (p + 1) * rows] = term.astype(terms.dtype)
        pairs = [(terms.at[k], outs[2 * g + k]) for k in range(2)]
        stores += start_all(pairs, sems, len(loads) + 2 * g)
    wait_all(stores)


def dx_terms(at, diffs, pieces):
    mb, toks, cols = diffs[0].shape
    part = toks // 2
    rows = pieces[0].shape[0]
    outs = four_terms(NC * mb * part, NX * rows)
    return pl.pallas_call(
        dx_body,
        out_shape=outs,
        in_specs=[SMEM, *([HBM] * (4 + NX))],
        out_specs=[HBM] * 4,
        scratch_shapes=[
            pltpu.VMEM((4, mb, toks, cols), BF16),
            pltpu.VMEM((4, NC, mb, part, cols), BF16),
            pltpu.VMEM((NX, rows, cols), BF16),
            pltpu.VMEM((2, NC * mb * part, NX * rows), BF16),
            pltpu.VMEM((2, NC * mb * part, NX * rows), F32),
            pltpu.SemaphoreType.DMA((12,)),
        ],
        compiler_params=pltpu.CompilerParams(vmem_limit_bytes=16 << 20),
        cost_estimate=cost(8 * math.prod(outs[0].shape) * cols, *outs, *diffs, *pieces),
        name="dx_terms",
    )(at, *map(in_hbm, (*diffs, *pieces)))


def place_body(at, keep_o, got_o, keep_p, got_p, out_ref):
    x, zh, c = at[0], at[1], at[2]
    mb, part, _ = out_ref.shape
    rows = keep_o.shape[-1] // NX
    for ref, z, n in (
        (keep_o, zh, c),
        (got_o, zh, 1 - c),
        (keep_p, 1 - zh, c),
        (got_p, 1 - zh, 1 - c),
    ):
        for p, away in enumerate(PIECES):
            start = ((((x + away) & (NX - 1)) * NZ + z) * NC + n) * rows
            lanes = pl.ds(pl.multiple_of(start, rows), rows)
            for m in range(mb):
                out_ref[m, :, lanes] = ref[
                    m * part : (m + 1) * part, p * rows : (p + 1) * rows
                ]


def place(at, mb, *parts):
    toks, width = parts[0].shape
    out = jax.ShapeDtypeStruct((mb, toks // mb, NZ * NC * width), BF16)
    vmem = pl.BlockSpec(memory_space=pltpu.VMEM)
    return pl.pallas_call(
        place_body,
        out_shape=out,
        in_specs=[pl.BlockSpec(memory_space=pltpu.SMEM), *([vmem] * 4)],
        out_specs=vmem,
        compiler_params=pltpu.CompilerParams(vmem_limit_bytes=8 << 20),
        cost_estimate=cost(0, out, out),
        name="place",
    )(at, *parts)


def after(value, *others):
    return lax.optimization_barrier((value, *others))[0]


def by_x(k):
    return [(x, (x + k) % NX) for x in range(NX)]


def by_core(n, way, core_first):
    def index(k, c):
        return c * n + k % n if core_first else (k % n) * NC + c

    return [
        (index(k, c), index(k + way * (1 - 2 * c), c)) for k in range(n) for c in range(NC)
    ]


SWAP = [(0, 1), (1, 0)]


def local(activations, student_out, teacher_out, weight):
    x, zh, c, y = (lax.axis_index(n) for n in ("x", "zh", "core", "outc"))
    zl = lax.axis_index("inc")
    d = 1 - 2 * c
    own = weight[0]
    mb = activations.shape[0]

    def step_x(value, way=1):
        return lax.ppermute(value, ("x", "core"), by_core(NX, way, False))

    def step_y(value, way=1):
        return lax.ppermute(value, ("core", "outc"), by_core(NY, way, True))

    def swap_zh(value):
        return lax.ppermute(value, "zh", SWAP)

    def swap_core(value):
        return lax.ppermute(value, "core", SWAP)

    def neighbours(piece):
        return lax.ppermute(piece, "x", by_x(1)), lax.ppermute(piece, "x", by_x(-1))

    def pick(below, above):
        return jnp.where(c == 0, below, above)

    ways = (2, -d, d, 0)
    at_o = jnp.stack([*(((x + k) & (NX - 1)) * NZ + zh for k in ways), c, zl])
    at_p = jnp.stack([*(((x + k) & (NX - 1)) * NZ + 1 - zh for k in ways), c, zl])

    def place_of(z, h):
        away = (2 * z + h - y) & (NY - 1)
        beside = jnp.where(away == (d & (NY - 1)), 2, 1)
        return jnp.where(away == 2, 0, jnp.where(away == 0, 3, beside))

    at_y = jnp.stack([place_of(z, h) for z in (zl, 1 - zl) for h in range(2)])

    diff = (student_out.astype(F32) - teacher_out.astype(F32)).astype(BF16)
    diff_z = lax.ppermute(diff, "inc", SWAP)
    diff_c = swap_core(diff)
    near_o = neighbours(after(own, diff))
    forward_o = pick(*near_o)
    far_o = step_x(forward_o)
    w_z = swap_zh(after(own, diff_z))
    diff_z = after(diff_z, diff_c, forward_o)
    diffs = (diff, diff_z, diff_c, swap_core(diff_z))
    act_got = swap_core(other_columns(after(activations, diff_z, far_o), c))

    def later(*others):
        return (after(diff, *others), *diffs[1:])

    def add(*terms):
        total = terms[0].astype(F32)
        for t in terms[1:]:
            total = total + t.astype(F32)
        return total

    def nearer(step, terms, *first):
        far, back, ahead, _ = terms
        far, back = lax.optimization_barrier((step(far), step(back, -1), *first))[:2]
        return add(ahead, far).astype(BF16), back

    terms_o = dx_terms(at_y, diffs, (own, *near_o, far_o))
    near_p = neighbours(after(w_z, terms_o[0]))
    sums_p = dw_terms(at_p, activations, act_got, later(*terms_o))
    next_dx_o, back_dx_o = nearer(step_y, terms_o, sums_p[0])
    forward_p = pick(after(near_p[0], sums_p[0]), near_p[1])
    sums_o = dw_terms(at_o, activations, act_got, later(forward_p, next_dx_o))
    next_p, back_p = nearer(step_x, sums_p, sums_o[0])
    far_p = step_x(forward_p)
    terms_p = dx_terms(at_y, later(*sums_o, next_p), (w_z, *near_p, far_p))
    dx_o = add(terms_o[3], back_dx_o, step_y(next_dx_o)).astype(BF16)
    whole_p = add(sums_p[3], back_p, step_x(next_p)).astype(BF16)
    next_o, back_o = nearer(step_x, sums_o, terms_p[0], whole_p)
    cross = swap_zh(whole_p)
    next_dx_p, back_dx_p = nearer(step_y, terms_p)
    dx_p = add(terms_p[3], back_dx_p, step_y(next_dx_p)).astype(BF16)
    weight_grad = add(sums_o[3], back_o, step_x(next_o), cross)

    half = dx_o.shape[0] // 2
    got_o, got_p = swap_core(dx_o[half:]), swap_core(dx_p[half:])
    input_grad = place(
        jnp.stack([x, zh, c]), mb, dx_o[:half], got_o, dx_p[:half], got_p
    )
    return input_grad, weight_grad.reshape(weight.shape)


def solution(mesh):
    fine = Mesh(
        mesh.devices.reshape(NX, NZ, NC, NL, NY), ("x", "zh", "core", "inc", "outc")
    )
    tok = ("x", "zh", "core")
    placed = (
        P(None, tok, "inc"),
        P(None, (*tok, "inc"), "outc"),
        P(None, (*tok, "inc"), "outc"),
        P("inc", tok, "outc"),
    )
    return jax.shard_map(
        local,
        mesh=fine,
        in_specs=placed,
        out_specs=(P(None, (*tok, "outc"), "inc"), P("inc", tok, "outc")),
        check_vma=False,
    )
```

```python
import math

import jax
import jax.numpy as jnp
from jax import lax
from jax.experimental import pallas as pl
from jax.experimental.pallas import tpu as pltpu
from jax.sharding import Mesh
from jax.sharding import PartitionSpec as P

NX, NZ, NC, NL, NY = 4, 2, 2, 2, 4
F32, BF16 = jnp.float32, jnp.bfloat16
PIECES = (0, -1, 1, 2)


def cost(flops, *arrays):
    moved = sum(math.prod(a.shape) * jnp.dtype(a.dtype).itemsize for a in arrays)
    return pl.CostEstimate(flops=flops, bytes_accessed=moved, transcendentals=0)


HBM = pl.BlockSpec(memory_space=pltpu.HBM)
SMEM = pl.BlockSpec(memory_space=pltpu.SMEM)


def in_hbm(array):
    return pltpu.with_memory_space_constraint(array, pltpu.HBM)


def start_all(pairs, sems, first=0):
    copies = [
        pltpu.make_async_copy(src, dst, sems.at[first + k])
        for k, (src, dst) in enumerate(pairs)
    ]
    for copy in copies:
        copy.start()
    return copies


def wait_all(copies):
    for copy in copies:
        copy.wait()


def other_columns(act, c):
    mb, toks, width = act.shape
    n = NX * NZ
    rows = width // (n * NC)

    def body(core, act_ref, out_ref, held, sems):
        loads = []
        for k in range(n):
            start = pl.multiple_of((k * NC + 1 - core[0]) * rows, rows)
            loads.append((act_ref.at[:, :, pl.ds(start, rows)], held.at[k]))
        stores = []
        for k, load in enumerate(start_all(loads, sems)):
            load.wait()
            stores += start_all([(held.at[k], out_ref.at[k])], sems, n + k)
        wait_all(stores)

    out = pltpu.HBM((n, mb, toks, rows), act.dtype)
    return pl.pallas_call(
        body,
        out_shape=out,
        in_specs=[SMEM, HBM],
        out_specs=HBM,
        scratch_shapes=[
            pltpu.VMEM((n, mb, toks, rows), act.dtype),
            pltpu.SemaphoreType.DMA((2 * n,)),
        ],
        compiler_params=pltpu.CompilerParams(vmem_limit_bytes=4 << 20),
        cost_estimate=cost(0, act, out),
        name="other_columns",
    )(c.reshape(1), in_hbm(act))


def four_terms(rows, cols):
    return [jax.ShapeDtypeStruct((rows, cols), BF16) for _ in range(4)]


def dw_body(at, act, got, mine, theirs, *refs):
    outs, held, sems = refs[:4], refs[4], refs[5]
    mb, toks, cols = mine.shape
    rows = got.shape[-1]
    step = cols // 2
    loads = []
    for k in range(4):
        start = pl.multiple_of((at[k] * NC + at[4]) * rows, rows)
        loads.append((act.at[:, :, pl.ds(start, rows)], held.at[k]))
    loads = start_all(loads, sems)

    def term(left, diff, j):
        return lax.dot_general(
            left.reshape(mb * toks, rows),
            diff[:, :, j : j + step].reshape(mb * toks, step),
            (((0,), (0,)), ((), ())),
            preferred_element_type=F32,
        )

    for k, out in enumerate(outs):
        for j in range(0, cols, step):
            total = term(got[at[k]], theirs, j)
            if j == 0:
                loads[k].wait()
            out[:, j : j + step] = (total + term(held[k], mine, j)).astype(out.dtype)


def dw_terms(at, act, got, mine, theirs):
    outs = four_terms(got.shape[-1], mine.shape[-1])
    vmem = pl.BlockSpec(memory_space=pltpu.VMEM)
    return pl.pallas_call(
        dw_body,
        out_shape=outs,
        in_specs=[SMEM, HBM, *([vmem] * 3)],
        out_specs=[vmem] * 4,
        scratch_shapes=[
            pltpu.VMEM((4, *got.shape[1:]), BF16),
            pltpu.SemaphoreType.DMA((4,)),
        ],
        compiler_params=pltpu.CompilerParams(vmem_limit_bytes=6 << 20),
        cost_estimate=cost(16 * mine.size * got.shape[-1], *outs, mine, theirs, got),
        name="dw_terms",
    )(at, in_hbm(act), got, mine, theirs)


def dx_body(at, mine, theirs, *refs):
    pieces, outs, lhs = refs[:NX], refs[NX : NX + 4], refs[NX + 4]
    mb, toks, cols = mine.shape
    part = toks // NY
    rows = pieces[0].shape[0]
    for k in range(4):
        start = pl.multiple_of(at[k] * part, part)
        for n, diff in enumerate((mine, theirs)):
            for m in range(mb):
                lhs[k, n, m] = diff[m, pl.ds(start, part)]
    each = NC * mb * part
    left = lhs[...].reshape(4 * each, cols)
    for p, piece in enumerate(pieces):
        got = lax.dot_general(
            left, piece[...], (((1,), (1,)), ((), ())), preferred_element_type=F32
        )
        for k, out in enumerate(outs):
            term = got[k * each : (k + 1) * each]
            out[:, p * rows : (p + 1) * rows] = term.astype(out.dtype)


def dx_terms(at, mine, theirs, pieces):
    mb, toks, cols = mine.shape
    part = toks // NY
    outs = four_terms(NC * mb * part, NX * pieces[0].shape[0])
    vmem = pl.BlockSpec(memory_space=pltpu.VMEM)
    return pl.pallas_call(
        dx_body,
        out_shape=outs,
        in_specs=[pl.BlockSpec(memory_space=pltpu.SMEM), *([vmem] * (2 + NX))],
        out_specs=[vmem] * 4,
        scratch_shapes=[pltpu.VMEM((4, NC, mb, part, cols), BF16)],
        compiler_params=pltpu.CompilerParams(vmem_limit_bytes=8 << 20),
        cost_estimate=cost(8 * math.prod(outs[0].shape) * cols, *outs, mine, theirs, *pieces),
        name="dx_terms",
    )(at, mine, theirs, *pieces)


def place_body(at, keep_o, got_o, keep_p, got_p, out_ref):
    x, zh, c = at[0], at[1], at[2]
    mb, part, _ = out_ref.shape
    rows = keep_o.shape[-1] // NX
    for ref, z, n in (
        (keep_o, zh, c),
        (got_o, zh, 1 - c),
        (keep_p, 1 - zh, c),
        (got_p, 1 - zh, 1 - c),
    ):
        for p, away in enumerate(PIECES):
            start = ((((x + away) & (NX - 1)) * NZ + z) * NC + n) * rows
            lanes = pl.ds(pl.multiple_of(start, rows), rows)
            for m in range(mb):
                out_ref[m, :, lanes] = ref[
                    m * part : (m + 1) * part, p * rows : (p + 1) * rows
                ]


def place(at, mb, *parts):
    toks, width = parts[0].shape
    out = jax.ShapeDtypeStruct((mb, toks // mb, NZ * NC * width), BF16)
    vmem = pl.BlockSpec(memory_space=pltpu.VMEM)
    return pl.pallas_call(
        place_body,
        out_shape=out,
        in_specs=[pl.BlockSpec(memory_space=pltpu.SMEM), *([vmem] * 4)],
        out_specs=vmem,
        compiler_params=pltpu.CompilerParams(vmem_limit_bytes=8 << 20),
        cost_estimate=cost(0, out, out),
        name="place",
    )(at, *parts)


def after(value, *others):
    return lax.optimization_barrier((value, *others))[0]


def by_x(k):
    return [(x, (x + k) % NX) for x in range(NX)]


def by_core(n, way, core_first):
    def index(k, c):
        return c * n + k % n if core_first else (k % n) * NC + c

    return [
        (index(k, c), index(k + way * (1 - 2 * c), c)) for k in range(n) for c in range(NC)
    ]


SWAP = [(0, 1), (1, 0)]


def local(activations, student_out, teacher_out, weight):
    x, zh, c, y = (lax.axis_index(n) for n in ("x", "zh", "core", "outc"))
    zl = lax.axis_index("inc")
    d = 1 - 2 * c
    own = weight[0]
    mb = activations.shape[0]

    def step_x(value, way=1):
        return lax.ppermute(value, ("x", "core"), by_core(NX, way, False))

    def step_y(value, way=1):
        return lax.ppermute(value, ("core", "outc"), by_core(NY, way, True))

    def swap_zh(value):
        return lax.ppermute(value, "zh", SWAP)

    def swap_core(value):
        return lax.ppermute(value, "core", SWAP)

    def neighbours(piece):
        return lax.ppermute(piece, "x", by_x(1)), lax.ppermute(piece, "x", by_x(-1))

    def pick(below, above):
        return jnp.where(c == 0, below, above)

    ways = (2, -d, d, 0)
    at_y = jnp.stack([(y + k) & (NY - 1) for k in ways])
    at_o = jnp.stack([*(((x + k) & (NX - 1)) * NZ + zh for k in ways), c])
    at_p = jnp.stack([*(((x + k) & (NX - 1)) * NZ + 1 - zh for k in ways), c])

    act_send = other_columns(activations, c)
    act_got = swap_core(act_send)
    student_out = after(student_out, act_send)
    diff = (student_out.astype(F32) - teacher_out.astype(F32)).astype(BF16)
    diff_z = lax.ppermute(diff, "inc", SWAP)
    near_o = neighbours(own)
    forward_o = pick(*near_o)
    far_o = step_x(forward_o)
    w_z = swap_zh(after(own, diff_z))
    diff_z = after(diff_z, forward_o)
    mine = jnp.where(
        zl == 0,
        jnp.concatenate([diff, diff_z], axis=1),
        jnp.concatenate([diff_z, diff], axis=1),
    )
    theirs = swap_core(mine)

    def add(*terms):
        total = terms[0].astype(F32)
        for t in terms[1:]:
            total = total + t.astype(F32)
        return total

    def nearer(step, terms, *first):
        far, back, ahead, _ = terms
        far, back = lax.optimization_barrier((step(far), step(back, -1), *first))[:2]
        return add(ahead, far).astype(BF16), back

    terms_o = dx_terms(at_y, mine, theirs, (own, *near_o, far_o))
    near_p = neighbours(after(w_z, terms_o[0]))
    sums_p = dw_terms(at_p, activations, act_got, mine, after(theirs, *terms_o))
    next_dx_o, back_dx_o = nearer(step_y, terms_o, sums_p[0])
    forward_p = pick(after(near_p[0], sums_p[0]), near_p[1])
    sums_o = dw_terms(at_o, activations, act_got, mine, after(theirs, forward_p, next_dx_o))
    next_p, back_p = nearer(step_x, sums_p, sums_o[0])
    far_p = step_x(forward_p)
    terms_p = dx_terms(at_y, mine, after(theirs, *sums_o, next_p), (w_z, *near_p, far_p))
    dx_o = add(terms_o[3], back_dx_o, step_y(next_dx_o)).astype(BF16)
    whole_p = add(sums_p[3], back_p, step_x(next_p)).astype(BF16)
    next_o, back_o = nearer(step_x, sums_o, terms_p[0], whole_p)
    cross = swap_zh(whole_p)
    next_dx_p, back_dx_p = nearer(step_y, terms_p)
    dx_p = add(terms_p[3], back_dx_p, step_y(next_dx_p)).astype(BF16)
    weight_grad = add(sums_o[3], back_o, step_x(next_o), cross)

    half = dx_o.shape[0] // 2
    got_o, got_p = swap_core(dx_o[half:]), swap_core(dx_p[half:])
    input_grad = place(
        jnp.stack([x, zh, c]), mb, dx_o[:half], got_o, dx_p[:half], got_p
    )
    return input_grad, weight_grad.reshape(weight.shape)


def solution(mesh):
    fine = Mesh(
        mesh.devices.reshape(NX, NZ, NC, NL, NY), ("x", "zh", "core", "inc", "outc")
    )
    tok = ("x", "zh", "core")
    placed = (
        P(None, tok, "inc"),
        P(None, (*tok, "inc"), "outc"),
        P(None, (*tok, "inc"), "outc"),
        P("inc", tok, "outc"),
    )
    return jax.shard_map(
        local,
        mesh=fine,
        in_specs=placed,
        out_specs=(P(None, (*tok, "outc"), "inc"), P("inc", tok, "outc")),
        check_vma=False,
    )
```

```python
import math

import jax
import jax.numpy as jnp
from jax import lax
from jax.experimental import pallas as pl
from jax.experimental.pallas import tpu as pltpu
from jax.sharding import Mesh
from jax.sharding import PartitionSpec as P

NX, NZ, NC, NL, NY = 4, 2, 2, 2, 4
F32, BF16 = jnp.float32, jnp.bfloat16
PIECES = (0, -1, 1, 2)


def cost(flops, *arrays):
    moved = sum(math.prod(a.shape) * jnp.dtype(a.dtype).itemsize for a in arrays)
    return pl.CostEstimate(flops=flops, bytes_accessed=moved, transcendentals=0)


HBM = pl.BlockSpec(memory_space=pltpu.HBM)
SMEM = pl.BlockSpec(memory_space=pltpu.SMEM)


def in_hbm(array):
    return pltpu.with_memory_space_constraint(array, pltpu.HBM)


def start_all(pairs, sems, first=0):
    copies = [
        pltpu.make_async_copy(src, dst, sems.at[first + k])
        for k, (src, dst) in enumerate(pairs)
    ]
    for copy in copies:
        copy.start()
    return copies


def wait_all(copies):
    for copy in copies:
        copy.wait()


def other_columns(act, c):
    mb, toks, width = act.shape
    n = NX * NZ
    rows = width // (n * NC)

    def body(core, act_ref, out_ref, held, sems):
        loads = []
        for k in range(n):
            start = pl.multiple_of((k * NC + 1 - core[0]) * rows, rows)
            loads.append((act_ref.at[:, :, pl.ds(start, rows)], held.at[k]))
        stores = []
        for k, load in enumerate(start_all(loads, sems)):
            load.wait()
            stores += start_all([(held.at[k], out_ref.at[k])], sems, n + k)
        wait_all(stores)

    out = pltpu.HBM((n, mb, toks, rows), act.dtype)
    return pl.pallas_call(
        body,
        out_shape=out,
        in_specs=[SMEM, HBM],
        out_specs=HBM,
        scratch_shapes=[
            pltpu.VMEM((n, mb, toks, rows), act.dtype),
            pltpu.SemaphoreType.DMA((2 * n,)),
        ],
        compiler_params=pltpu.CompilerParams(vmem_limit_bytes=4 << 20),
        cost_estimate=cost(0, act, out),
        name="other_columns",
    )(c.reshape(1), in_hbm(act))


def four_terms(rows, cols):
    return [jax.ShapeDtypeStruct((rows, cols), BF16) for _ in range(4)]


def dw_body(at, act, got, mine, theirs, *refs):
    outs, held, sems = refs[:4], refs[4], refs[5]
    mb, toks, cols = mine.shape
    rows = got.shape[-1]
    step = cols // 2
    loads = []
    for k in range(4):
        start = pl.multiple_of((at[k] * NC + at[4]) * rows, rows)
        loads.append((act.at[:, :, pl.ds(start, rows)], held.at[k]))
    loads = start_all(loads, sems)

    def term(left, diff, j):
        return lax.dot_general(
            left.reshape(mb * toks, rows),
            diff[:, :, j : j + step].reshape(mb * toks, step),
            (((0,), (0,)), ((), ())),
            preferred_element_type=F32,
        )

    for k, out in enumerate(outs):
        for j in range(0, cols, step):
            total = term(got[at[k]], theirs, j)
            if j == 0:
                loads[k].wait()
            out[:, j : j + step] = (total + term(held[k], mine, j)).astype(out.dtype)


def dw_terms(at, act, got, mine, theirs):
    outs = four_terms(got.shape[-1], mine.shape[-1])
    vmem = pl.BlockSpec(memory_space=pltpu.VMEM)
    return pl.pallas_call(
        dw_body,
        out_shape=outs,
        in_specs=[SMEM, HBM, *([vmem] * 3)],
        out_specs=[vmem] * 4,
        scratch_shapes=[
            pltpu.VMEM((4, *got.shape[1:]), BF16),
            pltpu.SemaphoreType.DMA((4,)),
        ],
        compiler_params=pltpu.CompilerParams(vmem_limit_bytes=6 << 20),
        cost_estimate=cost(16 * mine.size * got.shape[-1], *outs, mine, theirs, got),
        name="dw_terms",
    )(at, in_hbm(act), got, mine, theirs)


def dx_body(at, mine, theirs, *refs):
    pieces, outs, lhs = refs[:NX], refs[NX : NX + 4], refs[NX + 4]
    mb, toks, cols = mine.shape
    part = toks // NY
    rows = pieces[0].shape[0]
    for k in range(4):
        start = pl.multiple_of(at[k] * part, part)
        for n, diff in enumerate((mine, theirs)):
            for m in range(mb):
                lhs[k, n, m] = diff[m, pl.ds(start, part)]
    each = NC * mb * part
    left = lhs[...].reshape(4 * each, cols)
    for p, piece in enumerate(pieces):
        got = lax.dot_general(
            left, piece[...], (((1,), (1,)), ((), ())), preferred_element_type=F32
        )
        for k, out in enumerate(outs):
            term = got[k * each : (k + 1) * each]
            out[:, p * rows : (p + 1) * rows] = term.astype(out.dtype)


def dx_terms(at, mine, theirs, pieces):
    mb, toks, cols = mine.shape
    part = toks // NY
    outs = four_terms(NC * mb * part, NX * pieces[0].shape[0])
    vmem = pl.BlockSpec(memory_space=pltpu.VMEM)
    return pl.pallas_call(
        dx_body,
        out_shape=outs,
        in_specs=[pl.BlockSpec(memory_space=pltpu.SMEM), *([vmem] * (2 + NX))],
        out_specs=[vmem] * 4,
        scratch_shapes=[pltpu.VMEM((4, NC, mb, part, cols), BF16)],
        compiler_params=pltpu.CompilerParams(vmem_limit_bytes=8 << 20),
        cost_estimate=cost(8 * math.prod(outs[0].shape) * cols, *outs, mine, theirs, *pieces),
        name="dx_terms",
    )(at, mine, theirs, *pieces)


def place_body(at, keep_o, got_o, keep_p, got_p, out_ref):
    x, zh, c = at[0], at[1], at[2]
    mb, part, _ = out_ref.shape
    rows = keep_o.shape[-1] // NX
    for ref, z, n in (
        (keep_o, zh, c),
        (got_o, zh, 1 - c),
        (keep_p, 1 - zh, c),
        (got_p, 1 - zh, 1 - c),
    ):
        for p, away in enumerate(PIECES):
            start = ((((x + away) & (NX - 1)) * NZ + z) * NC + n) * rows
            lanes = pl.ds(pl.multiple_of(start, rows), rows)
            for m in range(mb):
                out_ref[m, :, lanes] = ref[
                    m * part : (m + 1) * part, p * rows : (p + 1) * rows
                ]


def place(at, mb, *parts):
    toks, width = parts[0].shape
    out = jax.ShapeDtypeStruct((mb, toks // mb, NZ * NC * width), BF16)
    vmem = pl.BlockSpec(memory_space=pltpu.VMEM)
    return pl.pallas_call(
        place_body,
        out_shape=out,
        in_specs=[pl.BlockSpec(memory_space=pltpu.SMEM), *([vmem] * 4)],
        out_specs=vmem,
        compiler_params=pltpu.CompilerParams(vmem_limit_bytes=8 << 20),
        cost_estimate=cost(0, out, out),
        name="place",
    )(at, *parts)


def after(value, *others):
    return lax.optimization_barrier((value, *others))[0]


def by_x(k):
    return [(x, (x + k) % NX) for x in range(NX)]


def by_core(n, way, core_first):
    def index(k, c):
        return c * n + k % n if core_first else (k % n) * NC + c

    return [
        (index(k, c), index(k + way * (1 - 2 * c), c)) for k in range(n) for c in range(NC)
    ]


SWAP = [(0, 1), (1, 0)]


def local(activations, student_out, teacher_out, weight):
    x, zh, c, y = (lax.axis_index(n) for n in ("x", "zh", "core", "outc"))
    zl = lax.axis_index("inc")
    d = 1 - 2 * c
    own = weight[0]
    mb = activations.shape[0]

    def step_x(value, way=1):
        return lax.ppermute(value, ("x", "core"), by_core(NX, way, False))

    def step_y(value, way=1):
        return lax.ppermute(value, ("core", "outc"), by_core(NY, way, True))

    def swap_zh(value):
        return lax.ppermute(value, "zh", SWAP)

    def swap_core(value):
        return lax.ppermute(value, "core", SWAP)

    def neighbours(piece):
        return lax.ppermute(piece, "x", by_x(1)), lax.ppermute(piece, "x", by_x(-1))

    def pick(below, above):
        return jnp.where(c == 0, below, above)

    ways = (2, -d, d, 0)
    at_y = jnp.stack([(y + k) & (NY - 1) for k in ways])
    at_o = jnp.stack([*(((x + k) & (NX - 1)) * NZ + zh for k in ways), c])
    at_p = jnp.stack([*(((x + k) & (NX - 1)) * NZ + 1 - zh for k in ways), c])

    act_send = other_columns(activations, c)
    act_got = swap_core(act_send)
    student_out = after(student_out, act_send)
    diff = (student_out.astype(F32) - teacher_out.astype(F32)).astype(BF16)
    diff_z = lax.ppermute(diff, "inc", SWAP)
    near_o = neighbours(own)
    forward_o = pick(*near_o)
    far_o = step_x(forward_o)
    w_z = swap_zh(after(own, diff_z))
    diff_z = after(diff_z, forward_o)
    mine = jnp.where(
        zl == 0,
        jnp.concatenate([diff, diff_z], axis=1),
        jnp.concatenate([diff_z, diff], axis=1),
    )
    theirs = swap_core(mine)

    def add(*terms):
        total = terms[0].astype(F32)
        for t in terms[1:]:
            total = total + t.astype(F32)
        return total

    def nearer(step, terms, *first):
        far, back, ahead, _ = terms
        far, back = lax.optimization_barrier((step(far), step(back, -1), *first))[:2]
        return add(ahead, far).astype(BF16), back

    terms_o = dx_terms(at_y, mine, theirs, (own, *near_o, far_o))
    near_p = neighbours(after(w_z, terms_o[0]))
    sums_p = dw_terms(at_p, activations, act_got, mine, after(theirs, *terms_o))
    next_dx_o, back_dx_o = nearer(step_y, terms_o, sums_p[0])
    forward_p = pick(after(near_p[0], sums_p[0]), near_p[1])
    sums_o = dw_terms(at_o, activations, act_got, mine, after(theirs, forward_p, next_dx_o))
    next_p, back_p = nearer(step_x, sums_p, sums_o[0])
    far_p = step_x(forward_p)
    dx_o = add(terms_o[3], back_dx_o, step_y(next_dx_o)).astype(BF16)
    terms_p = dx_terms(
        at_y, mine, after(theirs, *sums_o, next_p, dx_o), (w_z, *near_p, far_p)
    )
    whole_p = add(sums_p[3], back_p, step_x(next_p)).astype(BF16)
    next_o, back_o = nearer(step_x, sums_o, whole_p)
    cross = swap_zh(whole_p)
    next_dx_p, back_dx_p = nearer(step_y, terms_p, next_o, whole_p)
    weight_grad = add(sums_o[3], back_o, step_x(next_o), cross)
    last = after(step_y(next_dx_p), weight_grad)
    dx_p = add(terms_p[3], back_dx_p, last).astype(BF16)

    half = dx_o.shape[0] // 2
    got_o, got_p = swap_core(dx_o[half:]), swap_core(dx_p[half:])
    input_grad = place(
        jnp.stack([x, zh, c]), mb, dx_o[:half], got_o, dx_p[:half], got_p
    )
    return input_grad, weight_grad.reshape(weight.shape)


def solution(mesh):
    fine = Mesh(
        mesh.devices.reshape(NX, NZ, NC, NL, NY), ("x", "zh", "core", "inc", "outc")
    )
    tok = ("x", "zh", "core")
    placed = (
        P(None, tok, "inc"),
        P(None, (*tok, "inc"), "outc"),
        P(None, (*tok, "inc"), "outc"),
        P("inc", tok, "outc"),
    )
    return jax.shard_map(
        local,
        mesh=fine,
        in_specs=placed,
        out_specs=(P(None, (*tok, "outc"), "inc"), P("inc", tok, "outc")),
        check_vma=False,
    )
```

```python
import math

import jax
import jax.numpy as jnp
from jax import lax
from jax.experimental import pallas as pl
from jax.experimental.pallas import tpu as pltpu
from jax.sharding import Mesh
from jax.sharding import PartitionSpec as P

NX, NZ, NC, NL, NY = 4, 2, 2, 2, 4
F32, BF16 = jnp.float32, jnp.bfloat16
PIECES = (0, -1, 1, 2)


def cost(flops, *arrays):
    moved = sum(math.prod(a.shape) * jnp.dtype(a.dtype).itemsize for a in arrays)
    return pl.CostEstimate(flops=flops, bytes_accessed=moved, transcendentals=0)


HBM = pl.BlockSpec(memory_space=pltpu.HBM)
SMEM = pl.BlockSpec(memory_space=pltpu.SMEM)


def in_hbm(array):
    return pltpu.with_memory_space_constraint(array, pltpu.HBM)


def start_all(pairs, sems, first=0):
    copies = [
        pltpu.make_async_copy(src, dst, sems.at[first + k])
        for k, (src, dst) in enumerate(pairs)
    ]
    for copy in copies:
        copy.start()
    return copies


def wait_all(copies):
    for copy in copies:
        copy.wait()


def other_columns(act, c):
    mb, toks, width = act.shape
    n = NX * NZ
    rows = width // (n * NC)

    def body(core, act_ref, out_ref, held, sems):
        loads = []
        for k in range(n):
            start = pl.multiple_of((k * NC + 1 - core[0]) * rows, rows)
            loads.append((act_ref.at[:, :, pl.ds(start, rows)], held.at[k]))
        stores = []
        for k, load in enumerate(start_all(loads, sems)):
            load.wait()
            stores += start_all([(held.at[k], out_ref.at[k])], sems, n + k)
        wait_all(stores)

    out = pltpu.HBM((n, mb, toks, rows), act.dtype)
    return pl.pallas_call(
        body,
        out_shape=out,
        in_specs=[SMEM, HBM],
        out_specs=HBM,
        scratch_shapes=[
            pltpu.VMEM((n, mb, toks, rows), act.dtype),
            pltpu.SemaphoreType.DMA((2 * n,)),
        ],
        compiler_params=pltpu.CompilerParams(vmem_limit_bytes=4 << 20),
        cost_estimate=cost(0, act, out),
        name="other_columns",
    )(c.reshape(1), in_hbm(act))


def four_terms(rows, cols):
    return [jax.ShapeDtypeStruct((rows, cols), BF16) for _ in range(4)]


def dw_body(at, act, got, mine, theirs, *refs):
    outs, held, sems = refs[:4], refs[4], refs[5]
    mb, toks, cols = mine.shape
    rows = got.shape[-1]
    step = cols // 2
    loads = []
    for k in range(4):
        start = pl.multiple_of((at[k] * NC + at[4]) * rows, rows)
        loads.append((act.at[:, :, pl.ds(start, rows)], held.at[k]))
    loads = start_all(loads, sems)

    def term(left, diff, j):
        return lax.dot_general(
            left.reshape(mb * toks, rows),
            diff[:, :, j : j + step].reshape(mb * toks, step),
            (((0,), (0,)), ((), ())),
            preferred_element_type=F32,
        )

    for k, out in enumerate(outs):
        for j in range(0, cols, step):
            total = term(got[at[k]], theirs, j)
            if j == 0:
                loads[k].wait()
            out[:, j : j + step] = (total + term(held[k], mine, j)).astype(out.dtype)


def dw_terms(at, act, got, mine, theirs):
    outs = four_terms(got.shape[-1], mine.shape[-1])
    vmem = pl.BlockSpec(memory_space=pltpu.VMEM)
    return pl.pallas_call(
        dw_body,
        out_shape=outs,
        in_specs=[SMEM, HBM, *([vmem] * 3)],
        out_specs=[vmem] * 4,
        scratch_shapes=[
            pltpu.VMEM((4, *got.shape[1:]), BF16),
            pltpu.SemaphoreType.DMA((4,)),
        ],
        compiler_params=pltpu.CompilerParams(vmem_limit_bytes=6 << 20),
        cost_estimate=cost(16 * mine.size * got.shape[-1], *outs, mine, theirs, got),
        name="dw_terms",
    )(at, in_hbm(act), got, mine, theirs)


def dx_body(at, mine, theirs, *refs):
    pieces, outs, lhs, rhs, sems = refs[:NX], refs[NX : NX + 4], *refs[NX + 4 :]
    loads = start_all([(piece, rhs.at[p]) for p, piece in enumerate(pieces)], sems)
    mb, toks, cols = mine.shape
    part = toks // NY
    rows = pieces[0].shape[0]
    for k in range(4):
        start = pl.multiple_of(at[k] * part, part)
        for n, diff in enumerate((mine, theirs)):
            for m in range(mb):
                lhs[k, n, m] = diff[m, pl.ds(start, part)]
    each = NC * mb * part
    left = lhs[...].reshape(4 * each, cols)
    for p, load in enumerate(loads):
        load.wait()
        got = lax.dot_general(
            left, rhs[p], (((1,), (1,)), ((), ())), preferred_element_type=F32
        )
        for k, out in enumerate(outs):
            term = got[k * each : (k + 1) * each]
            out[:, p * rows : (p + 1) * rows] = term.astype(out.dtype)


def dx_terms(at, mine, theirs, pieces):
    mb, toks, cols = mine.shape
    part = toks // NY
    outs = four_terms(NC * mb * part, NX * pieces[0].shape[0])
    vmem = pl.BlockSpec(memory_space=pltpu.VMEM)
    return pl.pallas_call(
        dx_body,
        out_shape=outs,
        in_specs=[SMEM, vmem, vmem, *([HBM] * NX)],
        out_specs=[vmem] * 4,
        scratch_shapes=[
            pltpu.VMEM((4, NC, mb, part, cols), BF16),
            pltpu.VMEM((NX, *pieces[0].shape), BF16),
            pltpu.SemaphoreType.DMA((NX,)),
        ],
        compiler_params=pltpu.CompilerParams(vmem_limit_bytes=10 << 20),
        cost_estimate=cost(8 * math.prod(outs[0].shape) * cols, *outs, mine, theirs, *pieces),
        name="dx_terms",
    )(at, mine, theirs, *map(in_hbm, pieces))


def place_body(at, keep_o, got_o, keep_p, got_p, out_ref):
    x, zh, c = at[0], at[1], at[2]
    mb, part, _ = out_ref.shape
    rows = keep_o.shape[-1] // NX
    for ref, z, n in (
        (keep_o, zh, c),
        (got_o, zh, 1 - c),
        (keep_p, 1 - zh, c),
        (got_p, 1 - zh, 1 - c),
    ):
        for p, away in enumerate(PIECES):
            start = ((((x + away) & (NX - 1)) * NZ + z) * NC + n) * rows
            lanes = pl.ds(pl.multiple_of(start, rows), rows)
            for m in range(mb):
                out_ref[m, :, lanes] = ref[
                    m * part : (m + 1) * part, p * rows : (p + 1) * rows
                ]


def place(at, mb, *parts):
    toks, width = parts[0].shape
    out = jax.ShapeDtypeStruct((mb, toks // mb, NZ * NC * width), BF16)
    vmem = pl.BlockSpec(memory_space=pltpu.VMEM)
    return pl.pallas_call(
        place_body,
        out_shape=out,
        in_specs=[pl.BlockSpec(memory_space=pltpu.SMEM), *([vmem] * 4)],
        out_specs=vmem,
        compiler_params=pltpu.CompilerParams(vmem_limit_bytes=8 << 20),
        cost_estimate=cost(0, out, out),
        name="place",
    )(at, *parts)


def after(value, *others):
    return lax.optimization_barrier((value, *others))[0]


def by_x(k):
    return [(x, (x + k) % NX) for x in range(NX)]


def by_core(n, way, core_first):
    def index(k, c):
        return c * n + k % n if core_first else (k % n) * NC + c

    return [
        (index(k, c), index(k + way * (1 - 2 * c), c)) for k in range(n) for c in range(NC)
    ]


SWAP = [(0, 1), (1, 0)]


def local(activations, student_out, teacher_out, weight):
    x, zh, c, y = (lax.axis_index(n) for n in ("x", "zh", "core", "outc"))
    zl = lax.axis_index("inc")
    d = 1 - 2 * c
    own = weight[0]
    mb = activations.shape[0]

    def step_x(value, way=1):
        return lax.ppermute(value, ("x", "core"), by_core(NX, way, False))

    def step_y(value, way=1):
        return lax.ppermute(value, ("core", "outc"), by_core(NY, way, True))

    def swap_zh(value):
        return lax.ppermute(value, "zh", SWAP)

    def swap_core(value):
        return lax.ppermute(value, "core", SWAP)

    def neighbours(piece):
        return lax.ppermute(piece, "x", by_x(1)), lax.ppermute(piece, "x", by_x(-1))

    def pick(below, above):
        return jnp.where(c == 0, below, above)

    ways = (2, -d, d, 0)
    at_y = jnp.stack([(y + k) & (NY - 1) for k in ways])
    at_o = jnp.stack([*(((x + k) & (NX - 1)) * NZ + zh for k in ways), c])
    at_p = jnp.stack([*(((x + k) & (NX - 1)) * NZ + 1 - zh for k in ways), c])

    act_send = other_columns(activations, c)
    act_got = swap_core(act_send)
    student_out = after(student_out, act_send)
    diff = (student_out.astype(F32) - teacher_out.astype(F32)).astype(BF16)
    diff_z = lax.ppermute(diff, "inc", SWAP)
    near_o = neighbours(own)
    forward_o = pick(*near_o)
    far_o = step_x(forward_o)
    w_z = swap_zh(after(own, diff_z))
    diff_z = after(diff_z, far_o)
    mine = jnp.where(
        zl == 0,
        jnp.concatenate([diff, diff_z], axis=1),
        jnp.concatenate([diff_z, diff], axis=1),
    )
    theirs = swap_core(mine)

    def add(*terms):
        total = terms[0].astype(F32)
        for t in terms[1:]:
            total = total + t.astype(F32)
        return total

    def nearer(step, terms, *first):
        far, back, ahead, _ = terms
        far, back = lax.optimization_barrier((step(far), step(back, -1), *first))[:2]
        return add(ahead, far).astype(BF16), back

    terms_o = dx_terms(at_y, mine, theirs, (own, *near_o, far_o))
    near_p = neighbours(after(w_z, terms_o[0]))
    sums_p = dw_terms(at_p, activations, act_got, mine, after(theirs, *terms_o))
    next_dx_o, back_dx_o = nearer(step_y, terms_o, sums_p[0])
    forward_p = pick(after(near_p[0], sums_p[0]), near_p[1])
    sums_o = dw_terms(at_o, activations, act_got, mine, after(theirs, forward_p, next_dx_o))
    next_p, back_p = nearer(step_x, sums_p, sums_o[0])
    far_p = step_x(forward_p)
    dx_o = add(terms_o[3], back_dx_o, step_y(next_dx_o)).astype(BF16)
    terms_p = dx_terms(
        at_y, mine, after(theirs, *sums_o, next_p, dx_o), (w_z, *near_p, far_p)
    )
    whole_p = add(sums_p[3], back_p, step_x(next_p)).astype(BF16)
    next_o, back_o = nearer(step_x, sums_o, whole_p)
    cross = swap_zh(whole_p)
    next_dx_p, back_dx_p = nearer(step_y, terms_p, next_o, whole_p)
    weight_grad = add(sums_o[3], back_o, step_x(next_o), cross)
    last = after(step_y(next_dx_p), weight_grad)
    dx_p = add(terms_p[3], back_dx_p, last).astype(BF16)

    half = dx_o.shape[0] // 2
    got_o, got_p = swap_core(dx_o[half:]), swap_core(dx_p[half:])
    input_grad = place(
        jnp.stack([x, zh, c]), mb, dx_o[:half], got_o, dx_p[:half], got_p
    )
    return input_grad, weight_grad.reshape(weight.shape)


def solution(mesh):
    fine = Mesh(
        mesh.devices.reshape(NX, NZ, NC, NL, NY), ("x", "zh", "core", "inc", "outc")
    )
    tok = ("x", "zh", "core")
    placed = (
        P(None, tok, "inc"),
        P(None, (*tok, "inc"), "outc"),
        P(None, (*tok, "inc"), "outc"),
        P("inc", tok, "outc"),
    )
    return jax.shard_map(
        local,
        mesh=fine,
        in_specs=placed,
        out_specs=(P(None, (*tok, "outc"), "inc"), P("inc", tok, "outc")),
        check_vma=False,
    )
```

```python
import math

import jax
import jax.numpy as jnp
from jax import lax
from jax.experimental import pallas as pl
from jax.experimental.pallas import tpu as pltpu
from jax.sharding import Mesh
from jax.sharding import PartitionSpec as P

NX, NZ, NC, NL, NY = 4, 2, 2, 2, 4
F32, BF16 = jnp.float32, jnp.bfloat16
PIECES = (0, -1, 1, 2)


def cost(flops, *arrays):
    moved = sum(math.prod(a.shape) * jnp.dtype(a.dtype).itemsize for a in arrays)
    return pl.CostEstimate(flops=flops, bytes_accessed=moved, transcendentals=0)


HBM = pl.BlockSpec(memory_space=pltpu.HBM)
SMEM = pl.BlockSpec(memory_space=pltpu.SMEM)


def in_hbm(array):
    return pltpu.with_memory_space_constraint(array, pltpu.HBM)


def start_all(pairs, sems, first=0):
    copies = [
        pltpu.make_async_copy(src, dst, sems.at[first + k])
        for k, (src, dst) in enumerate(pairs)
    ]
    for copy in copies:
        copy.start()
    return copies


def wait_all(copies):
    for copy in copies:
        copy.wait()


def other_columns(act, c):
    mb, toks, width = act.shape
    n = NX * NZ
    rows = width // (n * NC)

    def body(core, act_ref, out_ref, held, sems):
        loads = []
        for k in range(n):
            start = pl.multiple_of((k * NC + 1 - core[0]) * rows, rows)
            loads.append((act_ref.at[:, :, pl.ds(start, rows)], held.at[k]))
        stores = []
        for k, load in enumerate(start_all(loads, sems)):
            load.wait()
            stores += start_all([(held.at[k], out_ref.at[k])], sems, n + k)
        wait_all(stores)

    out = pltpu.HBM((n, mb, toks, rows), act.dtype)
    return pl.pallas_call(
        body,
        out_shape=out,
        in_specs=[SMEM, HBM],
        out_specs=HBM,
        scratch_shapes=[
            pltpu.VMEM((n, mb, toks, rows), act.dtype),
            pltpu.SemaphoreType.DMA((2 * n,)),
        ],
        compiler_params=pltpu.CompilerParams(vmem_limit_bytes=4 << 20),
        cost_estimate=cost(0, act, out),
        name="other_columns",
    )(c.reshape(1), in_hbm(act))


def four_terms(rows, cols):
    return [jax.ShapeDtypeStruct((rows, cols), BF16) for _ in range(4)]


def dw_body(at, act, got, mine, theirs, *refs):
    outs, held, sems = refs[:4], refs[4], refs[5]
    mb, toks, cols = mine.shape
    rows = got.shape[-1]
    step = cols // 2
    loads = []
    for k in range(4):
        start = pl.multiple_of((at[k] * NC + at[4]) * rows, rows)
        loads.append((act.at[:, :, pl.ds(start, rows)], held.at[k]))
    loads = start_all(loads, sems)

    def term(left, diff, j):
        return lax.dot_general(
            left.reshape(mb * toks, rows),
            diff[:, :, j : j + step].reshape(mb * toks, step),
            (((0,), (0,)), ((), ())),
            preferred_element_type=F32,
        )

    for k, out in enumerate(outs):
        for j in range(0, cols, step):
            total = term(got[at[k]], theirs, j)
            if j == 0:
                loads[k].wait()
            out[:, j : j + step] = (total + term(held[k], mine, j)).astype(out.dtype)


def dw_terms(at, act, got, mine, theirs):
    outs = four_terms(got.shape[-1], mine.shape[-1])
    vmem = pl.BlockSpec(memory_space=pltpu.VMEM)
    return pl.pallas_call(
        dw_body,
        out_shape=outs,
        in_specs=[SMEM, HBM, *([vmem] * 3)],
        out_specs=[vmem] * 4,
        scratch_shapes=[
            pltpu.VMEM((4, *got.shape[1:]), BF16),
            pltpu.SemaphoreType.DMA((4,)),
        ],
        compiler_params=pltpu.CompilerParams(vmem_limit_bytes=6 << 20),
        cost_estimate=cost(16 * mine.size * got.shape[-1], *outs, mine, theirs, got),
        name="dw_terms",
    )(at, in_hbm(act), got, mine, theirs)


def dx_body(at, mine, theirs, *refs):
    pieces, outs, lhs = refs[:NX], refs[NX : NX + 4], refs[NX + 4]
    mb, toks, cols = mine.shape
    part = toks // NY
    rows = pieces[0].shape[0]
    for k in range(4):
        start = pl.multiple_of(at[k] * part, part)
        for n, diff in enumerate((mine, theirs)):
            for m in range(mb):
                lhs[k, n, m] = diff[m, pl.ds(start, part)]
    each = NC * mb * part
    left = lhs[...].reshape(4 * each, cols)
    for p, piece in enumerate(pieces):
        got = lax.dot_general(
            left, piece[...], (((1,), (1,)), ((), ())), preferred_element_type=F32
        )
        for k, out in enumerate(outs):
            term = got[k * each : (k + 1) * each]
            out[:, p * rows : (p + 1) * rows] = term.astype(out.dtype)


def dx_terms(at, mine, theirs, pieces):
    mb, toks, cols = mine.shape
    part = toks // NY
    outs = four_terms(NC * mb * part, NX * pieces[0].shape[0])
    vmem = pl.BlockSpec(memory_space=pltpu.VMEM)
    return pl.pallas_call(
        dx_body,
        out_shape=outs,
        in_specs=[pl.BlockSpec(memory_space=pltpu.SMEM), *([vmem] * (2 + NX))],
        out_specs=[vmem] * 4,
        scratch_shapes=[pltpu.VMEM((4, NC, mb, part, cols), BF16)],
        compiler_params=pltpu.CompilerParams(vmem_limit_bytes=8 << 20),
        cost_estimate=cost(8 * math.prod(outs[0].shape) * cols, *outs, mine, theirs, *pieces),
        name="dx_terms",
    )(at, mine, theirs, *pieces)


def place_body(at, keep_o, got_o, keep_p, got_p, out_ref):
    x, zh, c = at[0], at[1], at[2]
    mb, part, _ = out_ref.shape
    rows = keep_o.shape[-1] // NX
    for ref, z, n in (
        (keep_o, zh, c),
        (got_o, zh, 1 - c),
        (keep_p, 1 - zh, c),
        (got_p, 1 - zh, 1 - c),
    ):
        for p, away in enumerate(PIECES):
            start = ((((x + away) & (NX - 1)) * NZ + z) * NC + n) * rows
            lanes = pl.ds(pl.multiple_of(start, rows), rows)
            for m in range(mb):
                out_ref[m, :, lanes] = ref[
                    m * part : (m + 1) * part, p * rows : (p + 1) * rows
                ]


def place(at, mb, *parts):
    toks, width = parts[0].shape
    out = jax.ShapeDtypeStruct((mb, toks // mb, NZ * NC * width), BF16)
    vmem = pl.BlockSpec(memory_space=pltpu.VMEM)
    return pl.pallas_call(
        place_body,
        out_shape=out,
        in_specs=[pl.BlockSpec(memory_space=pltpu.SMEM), *([vmem] * 4)],
        out_specs=vmem,
        compiler_params=pltpu.CompilerParams(vmem_limit_bytes=8 << 20),
        cost_estimate=cost(0, out, out),
        name="place",
    )(at, *parts)


def after(value, *others):
    return lax.optimization_barrier((value, *others))[0]


def by_x(k):
    return [(x, (x + k) % NX) for x in range(NX)]


def by_core(n, way, core_first):
    def index(k, c):
        return c * n + k % n if core_first else (k % n) * NC + c

    return [
        (index(k, c), index(k + way * (1 - 2 * c), c)) for k in range(n) for c in range(NC)
    ]


SWAP = [(0, 1), (1, 0)]


def local(activations, student_out, teacher_out, weight):
    x, zh, c, y = (lax.axis_index(n) for n in ("x", "zh", "core", "outc"))
    zl = lax.axis_index("inc")
    d = 1 - 2 * c
    own = weight[0]
    mb = activations.shape[0]

    def step_x(value, way=1):
        return lax.ppermute(value, ("x", "core"), by_core(NX, way, False))

    def step_y(value, way=1):
        return lax.ppermute(value, ("core", "outc"), by_core(NY, way, True))

    def swap_zh(value):
        return lax.ppermute(value, "zh", SWAP)

    def swap_core(value):
        return lax.ppermute(value, "core", SWAP)

    def neighbours(piece):
        return lax.ppermute(piece, "x", by_x(1)), lax.ppermute(piece, "x", by_x(-1))

    def pick(below, above):
        return jnp.where(c == 0, below, above)

    ways = (2, -d, d, 0)
    at_y = jnp.stack([(y + k) & (NY - 1) for k in ways])
    at_o = jnp.stack([*(((x + k) & (NX - 1)) * NZ + zh for k in ways), c])
    at_p = jnp.stack([*(((x + k) & (NX - 1)) * NZ + 1 - zh for k in ways), c])

    act_send = other_columns(activations, c)
    act_got = swap_core(act_send)
    student_out = after(student_out, act_send)
    diff = (student_out.astype(F32) - teacher_out.astype(F32)).astype(BF16)
    diff_z = lax.ppermute(diff, "inc", SWAP)
    near_o = neighbours(own)
    forward_o = pick(*near_o)
    far_o = step_x(forward_o)
    w_z = swap_zh(after(own, diff_z))
    diff_z = after(diff_z, far_o)
    mine = jnp.where(
        zl == 0,
        jnp.concatenate([diff, diff_z], axis=1),
        jnp.concatenate([diff_z, diff], axis=1),
    )
    theirs = swap_core(mine)

    def add(*terms):
        total = terms[0].astype(F32)
        for t in terms[1:]:
            total = total + t.astype(F32)
        return total

    def nearer(step, terms, *first):
        far, back, ahead, _ = terms
        far, back = lax.optimization_barrier((step(far), step(back, -1), *first))[:2]
        return add(ahead, far).astype(BF16), back

    terms_o = dx_terms(at_y, mine, theirs, (own, *near_o, far_o))
    near_p = neighbours(after(w_z, terms_o[0]))
    sums_p = dw_terms(at_p, activations, act_got, mine, after(theirs, *terms_o))
    next_dx_o, back_dx_o = nearer(step_y, terms_o, sums_p[0])
    forward_p = pick(after(near_p[0], sums_p[0]), near_p[1])
    sums_o = dw_terms(at_o, activations, act_got, mine, after(theirs, forward_p, next_dx_o))
    next_p, back_p = nearer(step_x, sums_p, sums_o[0])
    far_p = step_x(forward_p)
    dx_o = add(terms_o[3], back_dx_o, step_y(next_dx_o)).astype(BF16)
    terms_p = dx_terms(
        at_y, mine, after(theirs, *sums_o, next_p, dx_o), (w_z, *near_p, far_p)
    )
    whole_p = add(sums_p[3], back_p, step_x(next_p)).astype(BF16)
    next_o, back_o = nearer(step_x, sums_o, whole_p)
    cross = swap_zh(whole_p)
    next_dx_p, back_dx_p = nearer(step_y, terms_p, next_o, whole_p)
    weight_grad = add(sums_o[3], back_o, step_x(next_o), cross)
    last = after(step_y(next_dx_p), weight_grad)
    dx_p = add(terms_p[3], back_dx_p, last).astype(BF16)

    half = dx_o.shape[0] // 2
    got_o, got_p = swap_core(dx_o[half:]), swap_core(dx_p[half:])
    input_grad = place(
        jnp.stack([x, zh, c]), mb, dx_o[:half], got_o, dx_p[:half], got_p
    )
    return input_grad, weight_grad.reshape(weight.shape)


def solution(mesh):
    fine = Mesh(
        mesh.devices.reshape(NX, NZ, NC, NL, NY), ("x", "zh", "core", "inc", "outc")
    )
    tok = ("x", "zh", "core")
    placed = (
        P(None, tok, "inc"),
        P(None, (*tok, "inc"), "outc"),
        P(None, (*tok, "inc"), "outc"),
        P("inc", tok, "outc"),
    )
    return jax.shard_map(
        local,
        mesh=fine,
        in_specs=placed,
        out_specs=(P(None, (*tok, "outc"), "inc"), P("inc", tok, "outc")),
        check_vma=False,
    )
```
